512 devices in a mesh: dp: 32 (over z, x_lo), mp: 16 (over x_hi, y, core).
Axes of the slice: x: 4 (x_hi: 2, x_lo: 2; x = x_hi * 2 + x_lo), y: 4, z: 16, core: 2. Of those that a mesh axis runs over, the one named last changes fastest.
Arguments:
- teacher_query: bfloat16 [2048, 8192], P('mp', 'dp'), may hold values from -120 to 120
- teacher_keys: bfloat16 [2048, 1024], P('mp'), may hold values from -6 to 6
- teacher_values: bfloat16 [2048, 1024], P('mp'), may hold values from -6 to 6
- teacher_out: bfloat16 [8192, 8192], P('dp', 'mp'), may hold values from -0.0625 to 0.0625
- teacher_resid: bfloat16 [2048, 8192], P('dp', 'mp'), may hold values from -1.5 to 1.5
- distill_proj: bfloat16 [8192, 4096], P('mp', 'dp'), may hold values from -1 to 2
- student_context: bfloat16 [2048, 4096], P('mp'), may hold values from -6 to 6
- student_resid: bfloat16 [2048, 4096], P('mp', 'dp'), may hold values from -3 to 3
- student_out: bfloat16 [4096, 4096], P(None, 'dp'), may hold values from -0.09375 to 0.09375
- student_gain: float32 [4096], replicated, may hold values from 0.5 to 1.5
Outputs:
- grad_wo: bfloat16 [4096, 4096], P(None, 'dp')
- grad_gain: float32 [4096], P('dp')
- grad_proj: float32 [8192, 4096], P('mp', 'dp')
The draws below stay inside these ranges and needn't reach their ends.
All inputs are finite; a program needn't handle non-finite values.
Results may differ from the reference program's by a relative error of at most 0.03.
Values may be sent and summed in bfloat16 or wider, within the bound.
No kernel may reach another device: no remote copies, remote signals or barrier semaphores. Data moves between devices by JAX's collectives and lax.ppermute only.
A program may use at most 64 MiB of HBM per device.

```python
import jax
import jax.numpy as jnp
from jax import lax

D_T = 8192
HEADS = 64
KV_HEADS = 8
HEAD = 128
D_S = 4096
TOKENS = 2048
N_DP = 32


def shared_keys(key):
    return jnp.clip(jax.random.normal(key, (TOKENS, KV_HEADS * HEAD), jnp.float32), -6.0, 6.0)


def shared_resid(key):
    source = jax.random.fold_in(key, 101)
    return jnp.clip(0.3 * jax.random.normal(source, (TOKENS, D_T), jnp.float32), -1.5, 1.5)


def draw_teacher_keys(key, part):
    keys = shared_keys(key)
    return keys.astype(jnp.bfloat16)


def draw_teacher_query(key, part):
    key = jax.random.fold_in(key, 23)
    base = jnp.clip(1.5 * jax.random.normal(key, (TOKENS, HEADS * HEAD), jnp.float32), -9.0, 9.0)
    return base.astype(jnp.bfloat16)


def draw_teacher_resid(key, part):
    return shared_resid(key).astype(jnp.bfloat16)


def draw_student_resid(key, part):
    resid = shared_resid(key)
    key = jax.random.fold_in(key, 37)
    noise = jax.random.normal(key, (TOKENS, D_S), jnp.float32)
    values = 3.3 * resid[:, :D_S] + 0.5 * noise
    return jnp.clip(values, -3.0, 3.0).astype(jnp.bfloat16)


def draw_distill_proj(key, part):
    key = jax.random.fold_in(key, 41)
    weights = jnp.clip(jax.random.normal(key, (D_T, D_S), jnp.float32), -6.0, 6.0) * D_T ** (-0.5)
    rows = lax.iota(jnp.int32, D_T)
    cols = lax.iota(jnp.int32, D_S)
    embed = rows[:, None] % D_S == cols[None, :]
    values = weights + jnp.where(embed, 1.5 * (D_S / D_T) ** 0.5, 0.0)
    return values.astype(jnp.bfloat16)


def level_of(rng, extent, shards, smallest, largest):
    gain = 1.0
    for axis_at, shards_of in shards:
        heights = jax.random.uniform(jax.random.fold_in(jax.random.fold_in(rng, 6), axis_at), (shards_of,), jnp.float32, smallest / len(shards), largest / len(shards))
        gain = gain * jnp.repeat(jnp.exp(heights), extent[axis_at] // shards_of).reshape((-1,) + (1,) * (len(extent) - 1 - axis_at))
    return gain


def scatter_about(own_key, dims, deviation, most, pieces=(), held_as=jnp.bfloat16):
    level = level_of(own_key, dims, pieces, -0.22, 0.18) if pieces else 1.0
    drawn = jax.random.normal(own_key, dims, jnp.float32) * deviation * level
    return jnp.minimum(jnp.maximum(drawn, -most), most).astype(held_as)


def setup_inputs(seed: int = 0) -> dict:
    splits = jax.random.split(jax.random.key(seed), 11)
    teacher_query = draw_teacher_query(jax.random.fold_in(splits[10], 71), 0)
    teacher_keys = draw_teacher_keys(jax.random.fold_in(splits[10], 71), 0)
    teacher_values = scatter_about(splits[2], (TOKENS, KV_HEADS * HEAD), 1.0, 6.0, ((0, 16),))
    teacher_out = scatter_about(splits[3], (D_T, D_T), D_T ** -0.5, 0.0625, ((0, 32), (1, 16)))
    teacher_resid = draw_teacher_resid(jax.random.fold_in(splits[10], 71), 0)
    distill_proj = draw_distill_proj(jax.random.fold_in(splits[10], 71), 0)
    student_context = scatter_about(splits[6], (TOKENS, D_S), 1.0, 6.0, ((0, 16),))
    student_resid = draw_student_resid(jax.random.fold_in(splits[10], 71), 0)
    student_out = scatter_about(splits[8], (D_S, D_S), D_S ** -0.5, 0.09375, ((1, 32),))
    student_gain = jnp.clip(1.0 + 0.1 * jax.random.normal(splits[9], (D_S,), jnp.float32), 0.5, 1.5)
    return {"teacher_query": teacher_query, "teacher_keys": teacher_keys, "teacher_values": teacher_values, "teacher_out": teacher_out, "teacher_resid": teacher_resid, "distill_proj": distill_proj, "student_context": student_context, "student_resid": student_resid, "student_out": student_out, "student_gain": student_gain}


EPS = 1e-05

def reference(teacher_query, teacher_keys, teacher_values, teacher_out, teacher_resid, distill_proj, student_context, student_resid, student_out, student_gain):
    groups = HEADS // KV_HEADS
    query_heads = teacher_query.reshape(TOKENS, HEADS, HEAD).transpose(1, 0, 2)
    key_heads = teacher_keys.reshape(TOKENS, KV_HEADS, HEAD).transpose(1, 0, 2)
    value_heads = teacher_values.reshape(TOKENS, KV_HEADS, HEAD).transpose(1, 0, 2)
    positions = lax.iota(jnp.int32, TOKENS)
    allowed = positions[:, None] >= positions[None, :]

    def one_head(index):
        query = lax.dynamic_index_in_dim(query_heads, index, 0, keepdims=False)
        shared = (index // groups).astype(jnp.int32)
        keys = lax.dynamic_index_in_dim(key_heads, shared, 0, keepdims=False)
        values = lax.dynamic_index_in_dim(value_heads, shared, 0, keepdims=False)
        scores = jnp.dot(query, keys.T, preferred_element_type=jnp.float32) * HEAD ** (-0.5)
        scores = jnp.where(allowed, scores, -jnp.inf)
        top = lax.optimization_barrier(jnp.max(scores, axis=1, keepdims=True))
        weights = jnp.exp(scores - top)
        probs = (weights / lax.optimization_barrier(jnp.sum(weights, axis=1, keepdims=True))).astype(jnp.bfloat16)
        return jnp.dot(probs, values, preferred_element_type=jnp.float32).astype(jnp.bfloat16)
    context = lax.map(one_head, jnp.arange(HEADS, dtype=jnp.int32))
    context = context.transpose(1, 0, 2).reshape(TOKENS, D_T)
    block = D_T // N_DP
    context_blocks = context.reshape(TOKENS, N_DP, block).transpose(1, 0, 2)
    out_blocks = teacher_out.reshape(N_DP, block, D_T)

    def add_block(total, pair):
        part = jnp.dot(pair[0], pair[1], preferred_element_type=jnp.float32).astype(jnp.bfloat16)
        part = lax.optimization_barrier(part)
        return (total + part.astype(jnp.float32), None)
    summed, _ = lax.scan(add_block, jnp.zeros((TOKENS, D_T), jnp.float32), (context_blocks, out_blocks))
    hidden = (teacher_resid.astype(jnp.float32) + summed).astype(jnp.bfloat16)
    target = jnp.dot(hidden, distill_proj, preferred_element_type=jnp.float32)
    state = student_resid.astype(jnp.float32) + jnp.dot(student_context, student_out, preferred_element_type=jnp.float32)
    inverse = lax.rsqrt(lax.optimization_barrier(jnp.mean(state * state, axis=1, keepdims=True)) + EPS)
    pred = state * inverse * student_gain
    error = (pred - target) * TOKENS ** (-0.5)
    upstream = error * student_gain
    inner = lax.optimization_barrier(jnp.mean(upstream * state, axis=1, keepdims=True))
    grad_state = inverse * upstream - state * inverse ** 3 * inner
    grad_wo = jnp.dot(student_context.T, grad_state.astype(jnp.bfloat16), preferred_element_type=jnp.float32).astype(jnp.bfloat16)
    grad_gain = lax.optimization_barrier(jnp.sum(error * state * inverse, axis=0))
    grad_proj = -jnp.dot(hidden.T, error.astype(jnp.bfloat16), preferred_element_type=jnp.float32)
    return (grad_wo, grad_gain, grad_proj)
```

```python
import jax
import jax.numpy as jnp
from jax import lax
from jax.sharding import Mesh
from jax.sharding import PartitionSpec as P

HEADS = 64
KV_HEADS = 8
HEAD = 128
EPS = 1e-05

DP = ("zh", "zl", "xl")
MP = ("xh", "y", "core")
NEAR = ("zl", "xl")
FAR = ("zh",)
AXES = DP + MP
SIZES = (4, 4, 2, 2, 4, 2)
N_FAR, N_NEAR, N_MP = 4, 8, 16

BF = jnp.bfloat16
F32 = jnp.float32


def exchange(pieces, axes):
    return lax.all_to_all(pieces, axes, 0, 0, tiled=True)


def to_all(block, axes, count):
    return exchange(jnp.broadcast_to(block[None], (count,) + block.shape), axes)


def on_device(
    teacher_query,
    teacher_keys,
    teacher_values,
    teacher_out,
    teacher_resid,
    distill_proj,
    student_context,
    student_resid,
    student_out,
    student_gain,
):
    far = lax.axis_index("zh")
    near = lax.axis_index(NEAR)
    dp_index = lax.axis_index(DP)
    mp_index = lax.axis_index(MP)
    rows, query_width = teacher_query.shape
    local_heads = query_width // HEAD
    total = rows * N_MP
    sub = rows // N_NEAR
    columns = student_out.shape[1]
    width = student_context.shape[1]
    d_cols = teacher_out.shape[1]
    head_rows = teacher_out.shape[0]

    packed = jnp.concatenate([teacher_out, teacher_resid], axis=0)
    packed_all = lax.all_gather(packed, NEAR, axis=0, tiled=False)
    out_near = packed_all[:, :head_rows].reshape(N_NEAR * head_rows, d_cols)
    resid_near = packed_all[:, head_rows:].reshape(N_FAR, N_NEAR, sub, d_cols)
    resid_mine = lax.dynamic_index_in_dim(resid_near, near, 1, keepdims=False)

    kv_start = dp_index * local_heads // (HEADS // KV_HEADS)
    key_mine = lax.dynamic_slice_in_dim(teacher_keys, kv_start * HEAD, HEAD, 1)
    value_mine = lax.dynamic_slice_in_dim(teacher_values, kv_start * HEAD, HEAD, 1)
    kv_all = to_all(jnp.concatenate([key_mine, value_mine], axis=1), MP, N_MP)
    kv_all = kv_all.reshape(total, 2 * HEAD)
    keyed = kv_all[:, :HEAD]
    valued = kv_all[:, HEAD:]
    queries = teacher_query.reshape(rows, local_heads, HEAD)
    scores = jnp.einsum(
        "qrd,kd->rqk", queries, keyed, preferred_element_type=F32
    ) * HEAD ** (-0.5)
    query_pos = mp_index * rows + lax.iota(jnp.int32, rows)
    key_pos = lax.iota(jnp.int32, total)
    allowed = query_pos[:, None] >= key_pos[None, :]
    scores = jnp.where(allowed, scores, -jnp.inf)
    top = jnp.max(scores, axis=-1, keepdims=True)
    weights = jnp.exp(scores - top)
    probs = (weights / jnp.sum(weights, axis=-1, keepdims=True)).astype(BF)
    context = jnp.einsum("rqk,kd->qrd", probs, valued, preferred_element_type=F32)
    context = context.astype(BF).reshape(N_NEAR, 1, sub, query_width)

    context = jnp.broadcast_to(context, (N_NEAR, N_MP, sub, query_width))
    context = exchange(
        context.reshape(N_NEAR * N_MP, sub, query_width), NEAR + MP
    ).reshape(N_NEAR, N_MP * sub, query_width)
    context = context.transpose(1, 0, 2).reshape(N_MP * sub, N_NEAR * query_width)
    head_terms = jnp.dot(context, out_near, preferred_element_type=F32).astype(BF)
    head_terms = exchange(
        head_terms.reshape(N_FAR, N_MP * sub // N_FAR, d_cols), FAR
    )
    summed = jnp.sum(head_terms.astype(F32), axis=0)
    resid_mine = resid_mine.reshape(N_MP * sub // N_FAR, d_cols).astype(F32)
    hidden = (resid_mine + summed).astype(BF)
    hidden_near = to_all(hidden, FAR, N_FAR).reshape(N_MP * sub, d_cols)

    proj_near = lax.all_gather(distill_proj, NEAR, axis=0, tiled=False)
    partial = jnp.einsum(
        "tk,gkc->tgc", hidden_near, proj_near, preferred_element_type=F32
    ).astype(BF)
    partial = exchange(partial.reshape(N_MP, sub, N_NEAR * columns), MP)
    target = jnp.sum(partial.astype(F32), axis=0)

    state = student_resid.astype(F32) + jnp.dot(
        student_context, student_out, preferred_element_type=F32
    )
    state = exchange(state.reshape(N_NEAR, sub, columns), NEAR)
    state = state.transpose(1, 0, 2).reshape(sub, N_NEAR * columns)
    gain = lax.dynamic_slice_in_dim(
        student_gain, far * N_NEAR * columns, N_NEAR * columns, 0
    )
    grad_scale = total ** (-0.5)
    gained = state * gain
    sums = jnp.stack(
        [
            jnp.sum(state * state, axis=1),
            jnp.sum(gained * gained, axis=1),
            jnp.sum(target * gained, axis=1),
        ]
    )
    sums = jnp.pad(sums, ((0, 5), (0, 128 - sub)))
    sums = jnp.sum(to_all(sums, FAR, N_FAR), axis=0)[:3, :sub]
    inverse = lax.rsqrt(sums[0] / width + EPS)
    inner = (inverse * sums[1] - sums[2]) * (grad_scale / width)
    inverse = inverse[:, None]
    error = (gained * inverse - target) * grad_scale
    grad_state = inverse * error * gain - state * (inverse**3 * inner[:, None])
    gain_part = jnp.sum(error * state * inverse, axis=0).reshape(N_NEAR, 1, columns)
    gain_high = gain_part.astype(BF)
    gain_low = (gain_part - gain_high.astype(F32)).astype(BF)

    def by_near(values):
        return values.reshape(sub, N_NEAR, columns).transpose(1, 0, 2)

    sent = jnp.concatenate(
        [
            by_near(error.astype(BF)),
            by_near(grad_state.astype(BF)),
            gain_high,
            gain_low,
            jnp.zeros((N_NEAR, 6, columns), BF),
        ],
        axis=1,
    )
    slab = sent.shape[1]
    sent = jnp.broadcast_to(sent[:, None], (N_NEAR, N_MP, slab, columns))
    got = exchange(sent.reshape(N_NEAR * N_MP, slab, columns), NEAR + MP)
    error_all = got[:, :sub].reshape(total, columns)
    grad_all = got[:, sub : 2 * sub].reshape(total, columns)
    grad_gain = jnp.sum(got[:, 2 * sub : 2 * sub + 2].astype(F32), axis=(0, 1))

    contract_rows = (((0,), (0,)), ((), ()))
    part = width // N_MP
    context_cols = exchange(
        student_context.reshape(rows, N_MP, part).transpose(1, 0, 2), MP
    )
    context_cols = context_cols.reshape(N_MP, N_NEAR, sub, part)
    context_cols = context_cols.transpose(1, 0, 2, 3).reshape(total, part)
    grad_wo = lax.dot_general(
        context_cols, grad_all, contract_rows, preferred_element_type=F32
    ).astype(BF)
    grad_wo = to_all(grad_wo, MP, N_MP).reshape(width, columns)

    hidden_all = lax.all_gather(hidden_near, NEAR, axis=0, tiled=True)
    grad_proj = -lax.dot_general(
        hidden_all, error_all, contract_rows, preferred_element_type=F32
    )
    return (grad_wo, grad_gain, grad_proj)


def solution(mesh):
    fine = Mesh(mesh.devices.reshape(SIZES), AXES)
    in_specs = (
        P(MP, DP),
        P(MP, None),
        P(MP, None),
        P(DP, MP),
        P(DP, MP),
        P(MP, DP),
        P(MP, None),
        P(MP, DP),
        P(None, DP),
        P(),
    )
    out_specs = (P(None, DP), P(DP), P(MP, DP))
    return jax.shard_map(
        on_device, mesh=fine, in_specs=in_specs, out_specs=out_specs, check_vma=False
    )
```

```python
import jax
import jax.numpy as jnp
from jax import lax
from jax.sharding import Mesh
from jax.sharding import PartitionSpec as P

HEADS = 64
KV_HEADS = 8
HEAD = 128
EPS = 1e-05

DP = ("zh", "zn", "xl")
MP = ("xh", "y", "core")
NEAR = ("zn",)
FAR = ("zh", "xl")
AXES = DP + MP
SIZES = (2, 8, 2, 2, 4, 2)
N_ZH, N_XL, N_FAR, N_NEAR, N_MP = 2, 2, 4, 8, 16

BF = jnp.bfloat16
F32 = jnp.float32


def exchange(pieces, axes):
    return lax.all_to_all(pieces, axes, 0, 0, tiled=True)


def to_all(block, axes, count):
    return exchange(jnp.broadcast_to(block[None], (count,) + block.shape), axes)


def split(values):
    high = values.astype(BF)
    return high, (values - high.astype(F32)).astype(BF)


def on_device(
    teacher_query,
    teacher_keys,
    teacher_values,
    teacher_out,
    teacher_resid,
    distill_proj,
    student_context,
    student_resid,
    student_out,
    student_gain,
):
    far = lax.axis_index(FAR)
    near = lax.axis_index(NEAR)
    dp_index = lax.axis_index(DP)
    mp_index = lax.axis_index(MP)
    rows, query_width = teacher_query.shape
    local_heads = query_width // HEAD
    total = rows * N_MP
    sub = rows // N_NEAR
    columns = student_out.shape[1]
    width = student_context.shape[1]
    head_rows, d_cols = teacher_out.shape
    resid_rows = teacher_resid.shape[0]
    few = sub // N_XL

    packed = jnp.concatenate(
        [teacher_out, teacher_resid, distill_proj.reshape(-1, d_cols)], axis=0
    )
    packed_all = lax.all_gather(packed, NEAR, axis=0, tiled=False)
    out_near = packed_all[:, :head_rows].reshape(N_NEAR * head_rows, d_cols)
    resid_near = packed_all[:, head_rows : head_rows + resid_rows]
    resid_near = resid_near.reshape(N_NEAR, N_NEAR, few, d_cols)
    resid_mine = lax.dynamic_index_in_dim(resid_near, near, 1, keepdims=False)
    proj_near = packed_all[:, head_rows + resid_rows :]
    proj_near = proj_near.reshape(N_NEAR, d_cols, columns)

    def by_near(values):
        values = values.reshape(N_XL, N_NEAR, few, values.shape[-1])
        return values.transpose(1, 0, 2, 3).reshape(N_NEAR, sub, values.shape[-1])

    kv_start = dp_index * local_heads // (HEADS // KV_HEADS)
    key_mine = lax.dynamic_slice_in_dim(teacher_keys, kv_start * HEAD, HEAD, 1)
    value_mine = lax.dynamic_slice_in_dim(teacher_values, kv_start * HEAD, HEAD, 1)
    kv_all = to_all(jnp.concatenate([key_mine, value_mine], axis=1), MP, N_MP)
    kv_all = kv_all.reshape(total, 2 * HEAD)
    keyed = kv_all[:, :HEAD]
    valued = kv_all[:, HEAD:]
    queries = teacher_query.reshape(rows, local_heads, HEAD)
    scores = jnp.einsum(
        "qrd,kd->rqk", queries, keyed, preferred_element_type=F32
    ) * HEAD ** (-0.5)
    query_pos = mp_index * rows + lax.iota(jnp.int32, rows)
    key_pos = lax.iota(jnp.int32, total)
    allowed = query_pos[:, None] >= key_pos[None, :]
    scores = jnp.where(allowed, scores, -jnp.inf)
    top = jnp.max(scores, axis=-1, keepdims=True)
    weights = jnp.exp(scores - top)
    probs = (weights / jnp.sum(weights, axis=-1, keepdims=True)).astype(BF)
    context = jnp.einsum("rqk,kd->qrd", probs, valued, preferred_element_type=F32)
    context = by_near(context.astype(BF).reshape(rows, query_width))

    state = student_resid.astype(F32) + jnp.dot(
        student_context, student_out, preferred_element_type=F32
    )
    gain = lax.dynamic_slice_in_dim(student_gain, dp_index * columns, columns, 0)

    state_high, state_low = split(state)
    state_parts = jnp.concatenate([state_high, state_low], axis=1)
    state_parts = by_near(state_parts)
    got = exchange(jnp.concatenate([context, state_parts], axis=1), NEAR)
    state_parts = got[:, sub:].astype(F32)
    state_wide = state_parts[:, :, :columns] + state_parts[:, :, columns:]
    context = got[:, :sub].transpose(1, 0, 2).reshape(sub, N_NEAR * query_width)
    context = to_all(context, MP, N_MP).reshape(N_MP * sub, N_NEAR * query_width)

    part = width // N_MP
    context_cols = exchange(
        student_context.reshape(rows, N_MP, part).transpose(1, 0, 2), MP
    ).reshape(total, part)
    context, context_cols = lax.optimization_barrier((context, context_cols))

    head_terms = jnp.dot(context, out_near, preferred_element_type=F32).astype(BF)
    head_terms = head_terms.reshape(N_ZH, N_NEAR, N_XL, few, d_cols)
    head_terms = head_terms.transpose(0, 2, 1, 3, 4)
    head_terms = exchange(
        head_terms.reshape(N_FAR, N_NEAR * few, d_cols), FAR
    )
    summed = jnp.sum(head_terms.astype(F32), axis=0)
    resid_mine = resid_mine.reshape(N_NEAR * few, d_cols).astype(F32)
    hidden = (resid_mine + summed).astype(BF)
    hidden_near = to_all(hidden, FAR, N_FAR)
    hidden_near = hidden_near.reshape(N_ZH, N_XL, N_NEAR, few, d_cols)
    hidden_near = hidden_near.transpose(0, 2, 1, 3, 4).reshape(N_MP * sub, d_cols)

    partial = jnp.einsum(
        "tk,gkc->tgc", hidden_near, proj_near, preferred_element_type=F32
    ).astype(BF)
    partial = exchange(partial.reshape(N_MP, sub, N_NEAR * columns), MP)
    target_wide = jnp.sum(partial.astype(F32), axis=0)
    target_wide = target_wide.reshape(sub, N_NEAR, columns).transpose(1, 0, 2)

    gain_wide = student_gain.reshape(N_ZH, N_NEAR, N_XL, columns)
    gain_wide = gain_wide.transpose(0, 2, 1, 3).reshape(N_FAR, N_NEAR, columns)
    gain_wide = lax.dynamic_index_in_dim(gain_wide, far, 0, keepdims=False)[:, None]
    gained = state_wide * gain_wide
    sums = jnp.stack(
        [
            jnp.sum(state_wide * state_wide, axis=(0, 2)),
            jnp.sum(gained * gained, axis=(0, 2)),
            jnp.sum(target_wide * gained, axis=(0, 2)),
        ]
    )
    sums = jnp.stack(split(sums)).reshape(1, 6 * sub)
    sums = jnp.pad(sums, ((0, 7), (0, columns - 6 * sub)))
    here = (lax.iota(jnp.int32, N_FAR) == far)[:, None, None, None]
    sent = jnp.where(here, target_wide.astype(BF)[None], jnp.zeros((), BF))
    sums = jnp.broadcast_to(sums, (N_FAR, N_NEAR, 8, columns))
    sent = jnp.concatenate([sent, sums], axis=2)
    sent = sent.reshape(N_ZH, N_XL, N_NEAR, sub + 8, columns)
    sent = sent.transpose(0, 2, 1, 3, 4)
    got = exchange(sent.reshape(N_FAR * N_NEAR, sub + 8, columns), DP)
    got = got.reshape(N_ZH, N_NEAR, N_XL, sub + 8, columns)
    got = jnp.sum(got.astype(F32), axis=(0, 2))
    target = got[:, :sub].reshape(N_NEAR, N_XL, few, columns)
    target = target.transpose(1, 0, 2, 3).reshape(rows, columns)
    sums = got[:, sub, : 6 * sub].reshape(N_NEAR, 2, 3, N_XL, few).sum(axis=1)
    sums = sums.transpose(1, 2, 0, 3).reshape(3, rows)

    grad_scale = total ** (-0.5)
    inverse = lax.rsqrt(sums[0] / width + EPS)
    inner = (inverse * sums[1] - sums[2]) * (grad_scale / width)
    inverse = inverse[:, None]
    error = (state * inverse * gain - target) * grad_scale
    grad_state = inverse * error * gain - state * (inverse**3 * inner[:, None])
    gain_part = jnp.sum(error * state * inverse, axis=0)[None]
    gain_part = jnp.pad(jnp.concatenate(split(gain_part), axis=1), ((0, 7), (0, 0)))
    sent = jnp.concatenate([error.astype(BF), grad_state.astype(BF)], axis=1)
    got = to_all(jnp.concatenate([sent, gain_part], axis=0), MP, N_MP)
    error_all = got[:, :rows, :columns]
    grad_all = got[:, :rows, columns:].reshape(total, columns)
    grad_gain = jnp.sum(got[:, rows].astype(F32), axis=0)
    grad_gain = grad_gain[:columns] + grad_gain[columns:]

    contract_rows = (((0,), (0,)), ((), ()))
    grad_wo = lax.dot_general(
        context_cols, grad_all, contract_rows, preferred_element_type=F32
    ).astype(BF)
    grad_wo = to_all(grad_wo, MP, N_MP).reshape(width, columns)

    hidden_all = lax.all_gather(hidden_near, NEAR, axis=0, tiled=True)
    error_all = error_all.reshape(N_MP, N_XL, N_NEAR, few, columns)
    error_all = error_all.transpose(2, 0, 1, 3, 4).reshape(total, columns)
    grad_proj = -lax.dot_general(
        hidden_all, error_all, contract_rows, preferred_element_type=F32
    )
    return (grad_wo, grad_gain, grad_proj)


def solution(mesh):
    fine = Mesh(mesh.devices.reshape(SIZES), AXES)
    in_specs = (
        P(MP, DP),
        P(MP, None),
        P(MP, None),
        P(DP, MP),
        P(DP, MP),
        P(MP, DP),
        P(MP, None),
        P(MP, DP),
        P(None, DP),
        P(),
    )
    out_specs = (P(None, DP), P(DP), P(MP, DP))
    return jax.shard_map(
        on_device, mesh=fine, in_specs=in_specs, out_specs=out_specs, check_vma=False
    )
```

```python
import functools

import jax
import jax.numpy as jnp
from jax import lax
from jax.experimental import pallas as pl
from jax.experimental.pallas import tpu as pltpu
from jax.sharding import Mesh
from jax.sharding import PartitionSpec as P

HEADS = 64
KV_HEADS = 8
HEAD = 128
EPS = 1e-05

DP = ("zn", "zf", "xl")
MP = ("xh", "y", "core")
NEAR = ("zn",)
FAR = ("zf", "xl")
AXES = DP + MP
N_NEAR, N_XL, N_MP = 8, 2, 16
N_ZF = 16 // N_NEAR
N_FAR = N_ZF * N_XL
SIZES = (N_NEAR, N_ZF, N_XL, 2, 4, 2)

BF = jnp.bfloat16
F32 = jnp.float32


def exchange(pieces, axes):
    return lax.all_to_all(pieces, axes, 0, 0, tiled=True)


def to_all(block, axes, count):
    return exchange(jnp.broadcast_to(block[None], (count,) + block.shape), axes)


def split(values):
    high = values.astype(BF)
    return high, (values - high.astype(F32)).astype(BF)


def head_sum_kernel(few, context_ref, out_ref, sum_ref, total):
    step = pl.program_id(0)
    context = context_ref[...]
    rows = context.shape[0] * context.shape[2]
    part = jnp.dot(
        context.reshape(rows, context.shape[3]),
        out_ref[0],
        preferred_element_type=F32,
    )

    @pl.when(step == 0)
    def _():
        total[...] = part

    @pl.when(step > 0)
    def _():
        total[...] += part

    @pl.when(step == N_NEAR - 1)
    def _():
        for far in range(N_FAR):
            pieces = []
            for block in range(N_NEAR):
                first = (block * N_FAR + far) * few
                pieces.append(total[first : first + few])
            sum_ref[far] = jnp.concatenate(pieces, axis=0).astype(BF)


def head_sum(context, packed, few, head_rows):
    n_mp, _, sub, features = context.shape
    d_cols = packed.shape[2]
    return pl.pallas_call(
        functools.partial(head_sum_kernel, few),
        grid=(N_NEAR,),
        in_specs=[
            pl.BlockSpec((n_mp, 1, sub, features), lambda g: (0, g, 0, 0)),
            pl.BlockSpec((1, head_rows, d_cols), lambda g: (g, 0, 0)),
        ],
        out_specs=pl.BlockSpec((N_FAR, N_NEAR * few, d_cols), lambda g: (0, 0, 0)),
        out_shape=jax.ShapeDtypeStruct((N_FAR, N_NEAR * few, d_cols), BF),
        scratch_shapes=[pltpu.VMEM((n_mp * sub, d_cols), F32)],
        compiler_params=pltpu.CompilerParams(vmem_limit_bytes=24 * 2**20),
        cost_estimate=pl.CostEstimate(
            flops=2 * n_mp * sub * features * N_NEAR * d_cols,
            bytes_accessed=4 * 2**20,
            transcendentals=0,
        ),
    )(context, packed)


def on_device(
    teacher_query,
    teacher_keys,
    teacher_values,
    teacher_out,
    teacher_resid,
    distill_proj,
    student_context,
    student_resid,
    student_out,
    student_gain,
):
    far = lax.axis_index(FAR)
    near = lax.axis_index(NEAR)
    dp_index = lax.axis_index(DP)
    mp_index = lax.axis_index(MP)
    rows, query_width = teacher_query.shape
    local_heads = query_width // HEAD
    total = rows * N_MP
    sub = rows // N_NEAR
    columns = student_out.shape[1]
    width = student_context.shape[1]
    head_rows, d_cols = teacher_out.shape
    resid_rows = teacher_resid.shape[0]
    few = sub // N_XL

    packed = jnp.concatenate(
        [teacher_out, teacher_resid, distill_proj.reshape(-1, d_cols)], axis=0
    )
    packed_all = lax.all_gather(packed, NEAR, axis=0, tiled=False)
    resid_near = packed_all[:, head_rows : head_rows + resid_rows]
    resid_near = resid_near.reshape(N_NEAR, N_NEAR, few, d_cols)
    resid_mine = lax.dynamic_index_in_dim(resid_near, near, 1, keepdims=False)
    proj_near = packed_all[:, head_rows + resid_rows :]
    proj_near = proj_near.reshape(N_NEAR, d_cols, columns)

    def by_near(values):
        values = values.reshape(N_XL, N_NEAR, few, values.shape[-1])
        return values.transpose(1, 0, 2, 3).reshape(N_NEAR, sub, values.shape[-1])

    kv_start = dp_index * local_heads // (HEADS // KV_HEADS)
    key_mine = lax.dynamic_slice_in_dim(teacher_keys, kv_start * HEAD, HEAD, 1)
    value_mine = lax.dynamic_slice_in_dim(teacher_values, kv_start * HEAD, HEAD, 1)
    kv_all = to_all(jnp.concatenate([key_mine, value_mine], axis=1), MP, N_MP)
    kv_all = kv_all.reshape(total, 2 * HEAD)
    keyed = kv_all[:, :HEAD]
    valued = kv_all[:, HEAD:]
    queries = teacher_query.reshape(rows, local_heads, HEAD)
    scores = jnp.einsum(
        "qrd,kd->rqk", queries, keyed, preferred_element_type=F32
    ) * HEAD ** (-0.5)
    query_pos = mp_index * rows + lax.iota(jnp.int32, rows)
    key_pos = lax.iota(jnp.int32, total)
    allowed = query_pos[:, None] >= key_pos[None, :]
    scores = jnp.where(allowed, scores, -jnp.inf)
    top = jnp.max(scores, axis=-1, keepdims=True)
    weights = jnp.exp(scores - top)
    probs = (weights / jnp.sum(weights, axis=-1, keepdims=True)).astype(BF)
    context = jnp.einsum("rqk,kd->qrd", probs, valued, preferred_element_type=F32)
    context = by_near(context.astype(BF).reshape(rows, query_width))

    state = student_resid.astype(F32) + jnp.dot(
        student_context, student_out, preferred_element_type=F32
    )
    gain = lax.dynamic_slice_in_dim(student_gain, dp_index * columns, columns, 0)

    state_high, state_low = split(state)
    state_parts = jnp.concatenate([state_high, state_low], axis=1)
    state_parts = by_near(state_parts)
    got = exchange(jnp.concatenate([context, state_parts], axis=1), NEAR)
    state_parts = got[:, sub:].astype(F32)
    state_wide = state_parts[:, :, :columns] + state_parts[:, :, columns:]
    part = width // N_MP
    context = got[:, :sub].reshape(rows, query_width)
    context = jnp.broadcast_to(context[None], (N_MP, rows, query_width))
    sent = student_context.reshape(rows, N_MP, part).transpose(1, 0, 2)
    got = exchange(jnp.concatenate([context, sent], axis=1), MP)
    context_cols = got[:, rows:].reshape(total, part)

    head_terms = head_sum(
        got.reshape(N_MP, 2 * N_NEAR, sub, query_width), packed_all, few, head_rows
    )
    head_terms = exchange(head_terms, FAR)
    summed = jnp.sum(head_terms.astype(F32), axis=0)
    resid_mine = resid_mine.reshape(N_NEAR * few, d_cols).astype(F32)
    hidden = (resid_mine + summed).astype(BF)
    hidden_near = to_all(hidden, FAR, N_FAR)
    hidden_near = hidden_near.reshape(N_FAR, N_NEAR, few, d_cols)
    hidden_near = hidden_near.transpose(1, 0, 2, 3).reshape(N_MP * sub, d_cols)

    partial = jnp.einsum(
        "tk,gkc->tgc", hidden_near, proj_near, preferred_element_type=F32
    ).astype(BF)
    partial = exchange(partial.reshape(N_MP, sub, N_NEAR * columns), MP)
    target_wide = jnp.sum(partial.astype(F32), axis=0)
    target_wide = target_wide.reshape(sub, N_NEAR, columns).transpose(1, 0, 2)

    gain_wide = student_gain.reshape(N_NEAR, N_FAR, columns)
    gain_wide = lax.dynamic_slice_in_dim(gain_wide, far, 1, 1)
    gained = state_wide * gain_wide
    sums = jnp.stack(
        [
            jnp.sum(state_wide * state_wide, axis=(0, 2)),
            jnp.sum(gained * gained, axis=(0, 2)),
            jnp.sum(target_wide * gained, axis=(0, 2)),
        ]
    )
    sums = jnp.stack(split(sums)).reshape(6 * sub)
    sums = jnp.pad(sums, (0, 8 * columns - 6 * sub)).reshape(8, columns)
    here = (lax.iota(jnp.int32, N_FAR) == far)[None, :, None, None]
    sent = jnp.where(here, target_wide.astype(BF)[:, None], jnp.zeros((), BF))
    sums = jnp.broadcast_to(sums, (N_NEAR, N_FAR, 8, columns))
    sent = jnp.concatenate([sent, sums], axis=2)
    got = exchange(sent.reshape(N_FAR * N_NEAR, sub + 8, columns), DP)
    got = got.reshape(N_NEAR, N_FAR, sub + 8, columns)
    got = jnp.sum(got.astype(F32), axis=1)
    target = got[:, :sub].reshape(N_NEAR, N_XL, few, columns)
    target = target.transpose(1, 0, 2, 3).reshape(rows, columns)
    sums = got[:, sub:].reshape(N_NEAR, 8 * columns)[:, : 6 * sub]
    sums = sums.reshape(N_NEAR, 2, 3, N_XL, few).sum(axis=1)
    sums = sums.transpose(1, 2, 0, 3).reshape(3, rows)

    grad_scale = total ** (-0.5)
    inverse = lax.rsqrt(sums[0] / width + EPS)
    inner = (inverse * sums[1] - sums[2]) * (grad_scale / width)
    inverse = inverse[:, None]
    error = (state * inverse * gain - target) * grad_scale
    grad_state = inverse * error * gain - state * (inverse**3 * inner[:, None])
    gain_part = jnp.sum(error * state * inverse, axis=0)[None]
    gain_part = jnp.pad(jnp.concatenate(split(gain_part), axis=1), ((0, 7), (0, 0)))
    sent = jnp.concatenate([error.astype(BF), grad_state.astype(BF)], axis=1)
    got = to_all(jnp.concatenate([sent, gain_part], axis=0), MP, N_MP)
    error_all = got[:, :rows, :columns]
    grad_all = got[:, :rows, columns:].reshape(total, columns)
    grad_gain = jnp.sum(got[:, rows].astype(F32), axis=0)
    grad_gain = grad_gain[:columns] + grad_gain[columns:]

    contract_rows = (((0,), (0,)), ((), ()))
    grad_wo = lax.dot_general(
        context_cols, grad_all, contract_rows, preferred_element_type=F32
    ).astype(BF)
    grad_wo = to_all(grad_wo, MP, N_MP).reshape(width, columns)

    hidden_all = lax.all_gather(hidden_near, NEAR, axis=0, tiled=True)
    error_all = error_all.reshape(N_MP, N_XL, N_NEAR, few, columns)
    error_all = error_all.transpose(2, 0, 1, 3, 4).reshape(total, columns)
    grad_proj = -lax.dot_general(
        hidden_all, error_all, contract_rows, preferred_element_type=F32
    )
    return (grad_wo, grad_gain, grad_proj)


def solution(mesh):
    fine = Mesh(mesh.devices.reshape(SIZES), AXES)
    in_specs = (
        P(MP, DP),
        P(MP, None),
        P(MP, None),
        P(DP, MP),
        P(DP, MP),
        P(MP, DP),
        P(MP, None),
        P(MP, DP),
        P(None, DP),
        P(),
    )
    out_specs = (P(None, DP), P(DP), P(MP, DP))
    return jax.shard_map(
        on_device, mesh=fine, in_specs=in_specs, out_specs=out_specs, check_vma=False
    )
```

```python
import functools

import jax
import jax.numpy as jnp
from jax import lax
from jax.experimental import pallas as pl
from jax.experimental.pallas import tpu as pltpu
from jax.sharding import Mesh
from jax.sharding import PartitionSpec as P

HEADS = 64
KV_HEADS = 8
HEAD = 128
EPS = 1e-05

DP = ("zn", "zf", "xl")
MP = ("xh", "y", "core")
NEAR = ("zn",)
FAR = ("zf", "xl")
AXES = DP + MP
N_NEAR, N_XL, N_MP = 8, 2, 16
N_ZF = 16 // N_NEAR
N_FAR = N_ZF * N_XL
AT_ONCE = 4
SIZES = (N_NEAR, N_ZF, N_XL, 2, 4, 2)

BF = jnp.bfloat16
F32 = jnp.float32


def exchange(pieces, axes):
    return lax.all_to_all(pieces, axes, 0, 0, tiled=True)


def to_all(block, axes, count):
    return exchange(jnp.broadcast_to(block[None], (count,) + block.shape), axes)


def split(values):
    high = values.astype(BF)
    return high, (values - high.astype(F32)).astype(BF)


def head_sum_kernel(few, context_ref, out_ref, sum_ref, total):
    step = pl.program_id(0)
    context = context_ref[...]
    rows = context.shape[0] * context.shape[2]
    part = sum(
        jnp.dot(
            context[:, device].reshape(rows, context.shape[3]),
            out_ref[device],
            preferred_element_type=F32,
        )
        for device in range(AT_ONCE)
    )

    @pl.when(step == 0)
    def _():
        total[...] = part

    @pl.when(step > 0)
    def _():
        total[...] += part

    @pl.when(step == N_NEAR // AT_ONCE - 1)
    def _():
        for far in range(N_FAR):
            pieces = []
            for block in range(N_NEAR):
                first = (block * N_FAR + far) * few
                pieces.append(total[first : first + few])
            sum_ref[far] = jnp.concatenate(pieces, axis=0).astype(BF)


def head_sum(context, packed, few, head_rows):
    n_mp, _, sub, features = context.shape
    d_cols = packed.shape[2]
    return pl.pallas_call(
        functools.partial(head_sum_kernel, few),
        grid=(N_NEAR // AT_ONCE,),
        in_specs=[
            pl.BlockSpec((n_mp, AT_ONCE, sub, features), lambda g: (0, g, 0, 0)),
            pl.BlockSpec((AT_ONCE, head_rows, d_cols), lambda g: (g, 0, 0)),
        ],
        out_specs=pl.BlockSpec((N_FAR, N_NEAR * few, d_cols), lambda g: (0, 0, 0)),
        out_shape=jax.ShapeDtypeStruct((N_FAR, N_NEAR * few, d_cols), BF),
        scratch_shapes=[pltpu.VMEM((n_mp * sub, d_cols), F32)],
        compiler_params=pltpu.CompilerParams(vmem_limit_bytes=60 * 2**20),
        cost_estimate=pl.CostEstimate(
            flops=2 * n_mp * sub * features * N_NEAR * d_cols,
            bytes_accessed=4 * 2**20,
            transcendentals=0,
        ),
    )(context, packed)


def project_kernel(hidden_ref, map_ref, out_ref, ordered):
    columns = out_ref.shape[2] // AT_ONCE

    @pl.when(pl.program_id(0) == 0)
    def _():
        few = hidden_ref.shape[1] // N_NEAR
        hidden = hidden_ref[...].astype(F32)
        pieces = []
        for block in range(N_NEAR):
            for far in range(N_FAR):
                pieces.append(hidden[far, block * few : (block + 1) * few])
        ordered[...] = jnp.concatenate(pieces, axis=0).astype(BF)

    folds = map_ref.shape[2] // columns
    for device in range(AT_ONCE):
        folded = map_ref[device]
        weights = jnp.concatenate(
            [folded[:, f * columns : (f + 1) * columns] for f in range(folds)], axis=0
        )
        part = jnp.dot(ordered[...], weights, preferred_element_type=F32)
        out_ref[:, :, device * columns : (device + 1) * columns] = part.astype(
            BF
        ).reshape(out_ref.shape[:2] + (columns,))


def project(hidden, packed, first, sub, columns):
    rows = hidden.shape[0] * hidden.shape[1]
    d_cols = hidden.shape[2]
    return pl.pallas_call(
        project_kernel,
        grid=(N_NEAR // AT_ONCE,),
        in_specs=[
            pl.BlockSpec(hidden.shape, lambda g: (0, 0, 0)),
            pl.BlockSpec((AT_ONCE, columns, d_cols), lambda g: (g, first // columns, 0)),
        ],
        out_specs=pl.BlockSpec(
            (rows // sub, sub, AT_ONCE * columns), lambda g: (0, 0, g)
        ),
        out_shape=jax.ShapeDtypeStruct((rows // sub, sub, N_NEAR * columns), BF),
        scratch_shapes=[pltpu.VMEM((rows, d_cols), BF)],
        compiler_params=pltpu.CompilerParams(vmem_limit_bytes=60 * 2**20),
        cost_estimate=pl.CostEstimate(
            flops=2 * rows * d_cols * N_NEAR * columns,
            bytes_accessed=2 * 2**20,
            transcendentals=0,
        ),
    )(hidden, packed)


def on_device(
    teacher_query,
    teacher_keys,
    teacher_values,
    teacher_out,
    teacher_resid,
    distill_proj,
    student_context,
    student_resid,
    student_out,
    student_gain,
):
    far = lax.axis_index(FAR)
    near = lax.axis_index(NEAR)
    dp_index = lax.axis_index(DP)
    mp_index = lax.axis_index(MP)
    rows, query_width = teacher_query.shape
    local_heads = query_width // HEAD
    total = rows * N_MP
    sub = rows // N_NEAR
    columns = student_out.shape[1]
    width = student_context.shape[1]
    head_rows, d_cols = teacher_out.shape
    few = sub // N_XL

    folds = d_cols // columns
    folded = distill_proj.reshape(folds, columns, columns)
    folded = folded.transpose(1, 0, 2).reshape(columns, d_cols)
    packed = jnp.concatenate([teacher_out, folded, teacher_resid], axis=0)
    packed_all = lax.all_gather(packed, NEAR, axis=0, tiled=False)
    resid_near = packed_all[:, head_rows + columns :]
    resid_near = resid_near.reshape(N_NEAR, N_NEAR, few, d_cols)
    resid_mine = lax.dynamic_index_in_dim(resid_near, near, 1, keepdims=False)

    def by_near(values):
        values = values.reshape(N_XL, N_NEAR, few, values.shape[-1])
        return values.transpose(1, 0, 2, 3).reshape(N_NEAR, sub, values.shape[-1])

    kv_start = dp_index * local_heads // (HEADS // KV_HEADS)
    key_mine = lax.dynamic_slice_in_dim(teacher_keys, kv_start * HEAD, HEAD, 1)
    value_mine = lax.dynamic_slice_in_dim(teacher_values, kv_start * HEAD, HEAD, 1)
    kv_all = to_all(jnp.concatenate([key_mine, value_mine], axis=1), MP, N_MP)
    kv_all = kv_all.reshape(total, 2 * HEAD)
    keyed = kv_all[:, :HEAD]
    valued = kv_all[:, HEAD:]
    queries = teacher_query.reshape(rows, local_heads, HEAD)
    scores = jnp.einsum(
        "qrd,kd->rqk", queries, keyed, preferred_element_type=F32
    ) * HEAD ** (-0.5)
    query_pos = mp_index * rows + lax.iota(jnp.int32, rows)
    key_pos = lax.iota(jnp.int32, total)
    allowed = query_pos[:, None] >= key_pos[None, :]
    scores = jnp.where(allowed, scores, -jnp.inf)
    top = jnp.max(scores, axis=-1, keepdims=True)
    weights = jnp.exp(scores - top)
    probs = (weights / jnp.sum(weights, axis=-1, keepdims=True)).astype(BF)
    context = jnp.einsum("rqk,kd->qrd", probs, valued, preferred_element_type=F32)
    context = by_near(context.astype(BF).reshape(rows, query_width))

    state = student_resid.astype(F32) + jnp.dot(
        student_context, student_out, preferred_element_type=F32
    )
    gain = lax.dynamic_slice_in_dim(student_gain, dp_index * columns, columns, 0)

    state_high, state_low = split(state)
    state_parts = jnp.concatenate([state_high, state_low], axis=1)
    state_parts = by_near(state_parts)
    got = exchange(jnp.concatenate([context, state_parts], axis=1), NEAR)
    state_parts = got[:, sub:].astype(F32)
    state_wide = state_parts[:, :, :columns] + state_parts[:, :, columns:]
    part = width // N_MP
    context = got[:, :sub].reshape(rows, query_width)
    context = jnp.broadcast_to(context[None], (N_MP, rows, query_width))
    sent = student_context.reshape(rows, N_MP, part).transpose(1, 0, 2)
    got = exchange(jnp.concatenate([context, sent], axis=1), MP)
    context_cols = got[:, rows:].reshape(total, part)

    head_terms = head_sum(
        got.reshape(N_MP, 2 * N_NEAR, sub, query_width), packed_all, few, head_rows
    )
    head_terms = exchange(head_terms, FAR)
    summed = jnp.sum(head_terms.astype(F32), axis=0)
    resid_mine = resid_mine.reshape(N_NEAR * few, d_cols).astype(F32)
    hidden = (resid_mine + summed).astype(BF)
    hidden_near = to_all(hidden, FAR, N_FAR)

    partial = exchange(project(hidden_near, packed_all, head_rows, sub, columns), MP)
    target_wide = jnp.sum(partial.astype(F32), axis=0)
    target_wide = target_wide.reshape(sub, N_NEAR, columns).transpose(1, 0, 2)

    gain_wide = student_gain.reshape(N_NEAR, N_FAR, columns)
    gain_wide = lax.dynamic_slice_in_dim(gain_wide, far, 1, 1)
    gained = state_wide * gain_wide
    sums = jnp.stack(
        [
            jnp.sum(state_wide * state_wide, axis=(0, 2)),
            jnp.sum(gained * gained, axis=(0, 2)),
            jnp.sum(target_wide * gained, axis=(0, 2)),
        ]
    )
    sums = jnp.stack(split(sums)).reshape(6 * sub)
    sums = jnp.pad(sums, (0, 8 * columns - 6 * sub)).reshape(8, columns)
    here = (lax.iota(jnp.int32, N_FAR) == far)[None, :, None, None]
    sent = jnp.where(here, target_wide.astype(BF)[:, None], jnp.zeros((), BF))
    sums = jnp.broadcast_to(sums, (N_NEAR, N_FAR, 8, columns))
    sent = jnp.concatenate([sent, sums], axis=2)
    got = exchange(sent.reshape(N_FAR * N_NEAR, sub + 8, columns), DP)
    got = got.reshape(N_NEAR, N_FAR, sub + 8, columns)
    got = jnp.sum(got.astype(F32), axis=1)
    target = got[:, :sub].reshape(N_NEAR, N_XL, few, columns)
    target = target.transpose(1, 0, 2, 3).reshape(rows, columns)
    sums = got[:, sub:].reshape(N_NEAR, 8 * columns)[:, : 6 * sub]
    sums = sums.reshape(N_NEAR, 2, 3, N_XL, few).sum(axis=1)
    sums = sums.transpose(1, 2, 0, 3).reshape(3, rows)

    grad_scale = total ** (-0.5)
    inverse = lax.rsqrt(sums[0] / width + EPS)
    inner = (inverse * sums[1] - sums[2]) * (grad_scale / width)
    inverse = inverse[:, None]
    error = (state * inverse * gain - target) * grad_scale
    grad_state = inverse * error * gain - state * (inverse**3 * inner[:, None])
    gain_part = jnp.sum(error * state * inverse, axis=0)[None]
    gain_part = jnp.pad(jnp.concatenate(split(gain_part), axis=1), ((0, 7), (0, 0)))
    sent = jnp.concatenate([error.astype(BF), grad_state.astype(BF)], axis=1)
    sent, context_cols = lax.optimization_barrier((sent, context_cols))
    got = to_all(jnp.concatenate([sent, gain_part], axis=0), MP, N_MP)
    error_all = got[:, :rows, :columns]
    grad_all = got[:, :rows, columns:].reshape(total, columns)
    grad_gain = jnp.sum(got[:, rows].astype(F32), axis=0)
    grad_gain = grad_gain[:columns] + grad_gain[columns:]

    contract_rows = (((0,), (0,)), ((), ()))
    grad_wo = lax.dot_general(
        context_cols, grad_all, contract_rows, preferred_element_type=F32
    ).astype(BF)
    grad_wo = to_all(grad_wo, MP, N_MP).reshape(width, columns)

    hidden_near = hidden_near.reshape(N_MP * sub, d_cols)
    hidden_all = lax.all_gather(hidden_near, NEAR, axis=0, tiled=True)
    error_all = error_all.reshape(N_NEAR, N_ZF, N_XL, N_NEAR, few, columns)
    error_all = error_all.transpose(3, 1, 2, 0, 4, 5).reshape(total, columns)
    grad_proj = -lax.dot_general(
        hidden_all, error_all, contract_rows, preferred_element_type=F32
    )
    return (grad_wo, grad_gain, grad_proj)


def solution(mesh):
    fine = Mesh(mesh.devices.reshape(SIZES), AXES)
    in_specs = (
        P(MP, DP),
        P(MP, None),
        P(MP, None),
        P(DP, MP),
        P(DP, MP),
        P(MP, DP),
        P(MP, None),
        P(MP, DP),
        P(None, DP),
        P(),
    )
    out_specs = (P(None, DP), P(DP), P(MP, DP))
    return jax.shard_map(
        on_device, mesh=fine, in_specs=in_specs, out_specs=out_specs, check_vma=False
    )
```

```python
import functools

import jax
import jax.numpy as jnp
from jax import lax
from jax.experimental import pallas as pl
from jax.experimental.pallas import tpu as pltpu
from jax.sharding import Mesh
from jax.sharding import PartitionSpec as P

HEADS = 64
KV_HEADS = 8
HEAD = 128
EPS = 1e-05

DP = ("zn", "zf", "xl")
MP = ("xh", "y", "core")
NEAR = ("zn",)
FAR = ("zf", "xl")
AXES = DP + MP
N_NEAR, N_XL, N_MP = 8, 2, 16
N_ZF = 16 // N_NEAR
N_FAR = N_ZF * N_XL
AT_ONCE = 4
SIZES = (N_NEAR, N_ZF, N_XL, 2, 4, 2)

BF = jnp.bfloat16
F32 = jnp.float32


def exchange(pieces, axes):
    return lax.all_to_all(pieces, axes, 0, 0, tiled=True)


def to_all(block, axes, count):
    return exchange(jnp.broadcast_to(block[None], (count,) + block.shape), axes)


def split(values):
    high = values.astype(BF)
    return high, (values - high.astype(F32)).astype(BF)


def head_sum_kernel(few, context_ref, out_ref, sum_ref, total):
    step = pl.program_id(0)
    context = context_ref[...]
    rows = context.shape[0] * context.shape[2]
    part = sum(
        jnp.dot(
            context[:, device].reshape(rows, context.shape[3]),
            out_ref[device],
            preferred_element_type=F32,
        )
        for device in range(AT_ONCE)
    )

    @pl.when(step == 0)
    def _():
        total[...] = part

    @pl.when(step > 0)
    def _():
        total[...] += part

    @pl.when(step == N_NEAR // AT_ONCE - 1)
    def _():
        for far in range(N_FAR):
            pieces = []
            for block in range(N_NEAR):
                first = (block * N_FAR + far) * few
                pieces.append(total[first : first + few])
            sum_ref[far] = jnp.concatenate(pieces, axis=0).astype(BF)


def head_sum(context, packed, few, head_rows):
    n_mp, _, sub, features = context.shape
    d_cols = packed.shape[2]
    return pl.pallas_call(
        functools.partial(head_sum_kernel, few),
        grid=(N_NEAR // AT_ONCE,),
        in_specs=[
            pl.BlockSpec((n_mp, AT_ONCE, sub, features), lambda g: (0, g, 0, 0)),
            pl.BlockSpec((AT_ONCE, head_rows, d_cols), lambda g: (g, 0, 0)),
        ],
        out_specs=pl.BlockSpec((N_FAR, N_NEAR * few, d_cols), lambda g: (0, 0, 0)),
        out_shape=jax.ShapeDtypeStruct((N_FAR, N_NEAR * few, d_cols), BF),
        scratch_shapes=[pltpu.VMEM((n_mp * sub, d_cols), F32)],
        compiler_params=pltpu.CompilerParams(vmem_limit_bytes=60 * 2**20),
        cost_estimate=pl.CostEstimate(
            flops=2 * n_mp * sub * features * N_NEAR * d_cols,
            bytes_accessed=4 * 2**20,
            transcendentals=0,
        ),
    )(context, packed)


def project_kernel(hidden_ref, map_ref, out_ref, ordered):
    columns = out_ref.shape[2] // AT_ONCE

    @pl.when(pl.program_id(0) == 0)
    def _():
        few = hidden_ref.shape[1] // N_NEAR
        hidden = hidden_ref[...].astype(F32)
        pieces = []
        for block in range(N_NEAR):
            for far in range(N_FAR):
                pieces.append(hidden[far, block * few : (block + 1) * few])
        ordered[...] = jnp.concatenate(pieces, axis=0).astype(BF)

    folds = map_ref.shape[2] // columns
    for device in range(AT_ONCE):
        folded = map_ref[device]
        weights = jnp.concatenate(
            [folded[:, f * columns : (f + 1) * columns] for f in range(folds)], axis=0
        )
        part = jnp.dot(ordered[...], weights, preferred_element_type=F32)
        out_ref[:, :, device * columns : (device + 1) * columns] = part.astype(
            BF
        ).reshape(out_ref.shape[:2] + (columns,))


def project(hidden, packed, first, sub, columns):
    rows = hidden.shape[0] * hidden.shape[1]
    d_cols = hidden.shape[2]
    return pl.pallas_call(
        project_kernel,
        grid=(N_NEAR // AT_ONCE,),
        in_specs=[
            pl.BlockSpec(hidden.shape, lambda g: (0, 0, 0)),
            pl.BlockSpec((AT_ONCE, columns, d_cols), lambda g: (g, first // columns, 0)),
        ],
        out_specs=pl.BlockSpec(
            (rows // sub, sub, AT_ONCE * columns), lambda g: (0, 0, g)
        ),
        out_shape=jax.ShapeDtypeStruct((rows // sub, sub, N_NEAR * columns), BF),
        scratch_shapes=[pltpu.VMEM((rows, d_cols), BF)],
        compiler_params=pltpu.CompilerParams(vmem_limit_bytes=60 * 2**20),
        cost_estimate=pl.CostEstimate(
            flops=2 * rows * d_cols * N_NEAR * columns,
            bytes_accessed=2 * 2**20,
            transcendentals=0,
        ),
    )(hidden, packed)


def attend_kernel(few, place_ref, query_ref, kv_ref, state_ref, out_ref):
    rows = query_ref.shape[0]
    heads = query_ref.shape[1] // HEAD
    total = kv_ref.shape[0] * kv_ref.shape[1]
    sub = N_XL * few
    kv = kv_ref[...].reshape(total, 2 * HEAD)
    keys, values = kv[:, :HEAD], kv[:, HEAD:]
    query_pos = place_ref[0] * rows + lax.broadcasted_iota(
        jnp.int32, (rows, total), 0
    )
    allowed = query_pos >= lax.broadcasted_iota(jnp.int32, (rows, total), 1)
    found = []
    for head in range(heads):
        scores = lax.dot_general(
            query_ref[:, head * HEAD : (head + 1) * HEAD],
            keys,
            (((1,), (1,)), ((), ())),
            preferred_element_type=F32,
        ) * HEAD ** (-0.5)
        scores = jnp.where(allowed, scores, -jnp.inf)
        weights = jnp.exp(scores - jnp.max(scores, axis=1, keepdims=True))
        probs = (weights / jnp.sum(weights, axis=1, keepdims=True)).astype(BF)
        found.append(jnp.dot(probs, values, preferred_element_type=F32))
    context = jnp.concatenate(found, axis=1)
    for device in range(N_NEAR):
        pieces = []
        for xl in range(N_XL):
            first = (xl * N_NEAR + device) * few
            pieces.append(context[first : first + few])
        out_ref[device, :sub] = jnp.concatenate(pieces, axis=0).astype(BF)
        out_ref[device, sub:] = state_ref[device]


def attend(place, query, kv, state_parts, few):
    near, sub, features = state_parts.shape
    total = kv.shape[0] * kv.shape[1]
    vmem = pl.BlockSpec(memory_space=pltpu.VMEM)
    return pl.pallas_call(
        functools.partial(attend_kernel, few),
        in_specs=[pl.BlockSpec(memory_space=pltpu.SMEM), vmem, vmem, vmem],
        out_specs=vmem,
        out_shape=jax.ShapeDtypeStruct((near, 2 * sub, features), BF),
        compiler_params=pltpu.CompilerParams(vmem_limit_bytes=40 * 2**20),
        cost_estimate=pl.CostEstimate(
            flops=4 * query.shape[0] * query.shape[1] * total,
            bytes_accessed=2 * 2**20,
            transcendentals=query.shape[0] * query.shape[1] // HEAD * total,
        ),
    )(place, query, kv, state_parts)


def weight_kernel(context_ref, grad_ref, out_ref):
    blocks, rows, part = context_ref.shape
    columns = out_ref.shape[2]
    grad = lax.dot_general(
        context_ref[...].reshape(blocks * rows, part),
        grad_ref[:, :, columns:].reshape(blocks * rows, columns),
        (((0,), (0,)), ((), ())),
        preferred_element_type=F32,
    )
    out_ref[...] = jnp.broadcast_to(grad.astype(BF)[None], out_ref.shape)


def weight_grad(got, sent, rows, columns):
    blocks, _, part = got.shape
    return pl.pallas_call(
        weight_kernel,
        grid=(1,),
        in_specs=[
            pl.BlockSpec((blocks, rows, part), lambda g: (0, 1, 0)),
            pl.BlockSpec((blocks, rows, 2 * columns), lambda g: (0, 0, 0)),
        ],
        out_specs=pl.BlockSpec((blocks, part, columns), lambda g: (0, 0, 0)),
        out_shape=jax.ShapeDtypeStruct((blocks, part, columns), BF),
        compiler_params=pltpu.CompilerParams(vmem_limit_bytes=40 * 2**20),
        cost_estimate=pl.CostEstimate(
            flops=2 * blocks * rows * part * columns,
            bytes_accessed=3 * 2**20,
            transcendentals=0,
        ),
    )(got, sent)


def on_device(
    teacher_query,
    teacher_keys,
    teacher_values,
    teacher_out,
    teacher_resid,
    distill_proj,
    student_context,
    student_resid,
    student_out,
    student_gain,
):
    far = lax.axis_index(FAR)
    near = lax.axis_index(NEAR)
    dp_index = lax.axis_index(DP)
    mp_index = lax.axis_index(MP)
    rows, query_width = teacher_query.shape
    local_heads = query_width // HEAD
    total = rows * N_MP
    sub = rows // N_NEAR
    columns = student_out.shape[1]
    width = student_context.shape[1]
    head_rows, d_cols = teacher_out.shape
    few = sub // N_XL

    folds = d_cols // columns
    folded = distill_proj.reshape(folds, columns, columns)
    folded = folded.transpose(1, 0, 2).reshape(columns, d_cols)
    packed = jnp.concatenate([teacher_out, folded, teacher_resid], axis=0)
    packed_all = lax.all_gather(packed, NEAR, axis=0, tiled=False)
    resid_near = packed_all[:, head_rows + columns :]
    resid_near = resid_near.reshape(N_NEAR, N_NEAR, few, d_cols)
    resid_mine = lax.dynamic_index_in_dim(resid_near, near, 1, keepdims=False)

    def by_near(values):
        values = values.reshape(N_XL, N_NEAR, few, values.shape[-1])
        return values.transpose(1, 0, 2, 3).reshape(N_NEAR, sub, values.shape[-1])

    kv_start = dp_index * local_heads // (HEADS // KV_HEADS)
    key_mine = lax.dynamic_slice_in_dim(teacher_keys, kv_start * HEAD, HEAD, 1)
    value_mine = lax.dynamic_slice_in_dim(teacher_values, kv_start * HEAD, HEAD, 1)
    kv_all = to_all(jnp.concatenate([key_mine, value_mine], axis=1), MP, N_MP)
    state = student_resid.astype(F32) + jnp.dot(
        student_context, student_out, preferred_element_type=F32
    )
    gain = lax.dynamic_slice_in_dim(student_gain, dp_index * columns, columns, 0)

    state_high, state_low = split(state)
    state_parts = jnp.concatenate([state_high, state_low], axis=1)
    state_parts = by_near(state_parts)
    place = jnp.full((1,), mp_index, jnp.int32)
    got = exchange(attend(place, teacher_query, kv_all, state_parts, few), NEAR)
    state_parts = got[:, sub:].astype(F32)
    state_wide = state_parts[:, :, :columns] + state_parts[:, :, columns:]
    part = width // N_MP
    context = got[:, :sub].reshape(rows, query_width)
    context = jnp.broadcast_to(context[None], (N_MP, rows, query_width))
    sent = student_context.reshape(rows, N_MP, part).transpose(1, 0, 2)
    got = exchange(jnp.concatenate([context, sent], axis=1), MP)
    context_cols = got

    head_terms = head_sum(
        got.reshape(N_MP, 2 * N_NEAR, sub, query_width), packed_all, few, head_rows
    )
    head_terms = exchange(head_terms, FAR)
    summed = jnp.sum(head_terms.astype(F32), axis=0)
    resid_mine = resid_mine.reshape(N_NEAR * few, d_cols).astype(F32)
    hidden = (resid_mine + summed).astype(BF)
    hidden_near = to_all(hidden, FAR, N_FAR)

    partial = exchange(project(hidden_near, packed_all, head_rows, sub, columns), MP)
    target_wide = jnp.sum(partial.astype(F32), axis=0)
    target_wide = target_wide.reshape(sub, N_NEAR, columns).transpose(1, 0, 2)

    gain_wide = student_gain.reshape(N_NEAR, N_FAR, columns)
    gain_wide = lax.dynamic_slice_in_dim(gain_wide, far, 1, 1)
    gained = state_wide * gain_wide
    sums = jnp.stack(
        [
            jnp.sum(state_wide * state_wide, axis=(0, 2)),
            jnp.sum(gained * gained, axis=(0, 2)),
            jnp.sum(target_wide * gained, axis=(0, 2)),
        ]
    )
    sums = jnp.stack(split(sums)).reshape(6 * sub)
    sums = jnp.pad(sums, (0, 8 * columns - 6 * sub)).reshape(8, columns)
    here = (lax.iota(jnp.int32, N_FAR) == far)[None, :, None, None]
    sent = jnp.where(here, target_wide.astype(BF)[:, None], jnp.zeros((), BF))
    sums = jnp.broadcast_to(sums, (N_NEAR, N_FAR, 8, columns))
    sent = jnp.concatenate([sent, sums], axis=2)
    got = exchange(sent.reshape(N_FAR * N_NEAR, sub + 8, columns), DP)
    got = got.reshape(N_NEAR, N_FAR, sub + 8, columns)
    got = jnp.sum(got.astype(F32), axis=1)
    target = got[:, :sub].reshape(N_NEAR, N_XL, few, columns)
    target = target.transpose(1, 0, 2, 3).reshape(rows, columns)
    sums = got[:, sub:].reshape(N_NEAR, 8 * columns)[:, : 6 * sub]
    sums = sums.reshape(N_NEAR, 2, 3, N_XL, few).sum(axis=1)
    sums = sums.transpose(1, 2, 0, 3).reshape(3, rows)

    grad_scale = total ** (-0.5)
    inverse = lax.rsqrt(sums[0] / width + EPS)
    inner = (inverse * sums[1] - sums[2]) * (grad_scale / width)
    inverse = inverse[:, None]
    error = (state * inverse * gain - target) * grad_scale
    grad_state = inverse * error * gain - state * (inverse**3 * inner[:, None])
    gain_part = jnp.sum(error * state * inverse, axis=0)[None]
    gain_part = jnp.pad(jnp.concatenate(split(gain_part), axis=1), ((0, 7), (0, 0)))
    sent = jnp.concatenate([error.astype(BF), grad_state.astype(BF)], axis=1)
    got = to_all(jnp.concatenate([sent, gain_part], axis=0), MP, N_MP)
    error_all = got[:, :rows, :columns]
    grad_gain = jnp.sum(got[:, rows].astype(F32), axis=0)
    grad_gain = grad_gain[:columns] + grad_gain[columns:]

    contract_rows = (((0,), (0,)), ((), ()))
    grad_wo = weight_grad(context_cols, got, rows, columns)
    grad_wo = exchange(grad_wo, MP).reshape(width, columns)

    hidden_near = hidden_near.reshape(N_MP * sub, d_cols)
    hidden_all = lax.all_gather(hidden_near, NEAR, axis=0, tiled=True)
    error_all = error_all.reshape(N_NEAR, N_ZF, N_XL, N_NEAR, few, columns)
    error_all = error_all.transpose(3, 1, 2, 0, 4, 5).reshape(total, columns)
    grad_proj = -lax.dot_general(
        hidden_all, error_all, contract_rows, preferred_element_type=F32
    )
    grad_wo, grad_proj = lax.optimization_barrier((grad_wo, grad_proj))
    return (grad_wo, grad_gain, grad_proj)


def solution(mesh):
    fine = Mesh(mesh.devices.reshape(SIZES), AXES)
    in_specs = (
        P(MP, DP),
        P(MP, None),
        P(MP, None),
        P(DP, MP),
        P(DP, MP),
        P(MP, DP),
        P(MP, None),
        P(MP, DP),
        P(None, DP),
        P(),
    )
    out_specs = (P(None, DP), P(DP), P(MP, DP))
    return jax.shard_map(
        on_device, mesh=fine, in_specs=in_specs, out_specs=out_specs, check_vma=False
    )
```

```python
import functools

import jax
import jax.numpy as jnp
from jax import lax
from jax.experimental import pallas as pl
from jax.experimental.pallas import tpu as pltpu
from jax.sharding import Mesh
from jax.sharding import PartitionSpec as P

HEADS = 64
KV_HEADS = 8
HEAD = 128
EPS = 1e-05

DP = ("zn", "zf", "xl")
MP = ("xh", "y", "core")
NEAR = ("zn",)
FAR = ("zf", "xl")
AXES = DP + MP
N_NEAR, N_XL, N_MP = 8, 2, 16
N_ZF = 16 // N_NEAR
N_FAR = N_ZF * N_XL
AT_ONCE = 4
SIZES = (N_NEAR, N_ZF, N_XL, 2, 4, 2)

BF = jnp.bfloat16
F32 = jnp.float32


def exchange(pieces, axes):
    return lax.all_to_all(pieces, axes, 0, 0, tiled=True)


def to_all(block, axes, count):
    return exchange(jnp.broadcast_to(block[None], (count,) + block.shape), axes)


def split(values):
    high = values.astype(BF)
    return high, (values - high.astype(F32)).astype(BF)


def head_sum_kernel(few, context_ref, out_ref, sum_ref, total):
    step = pl.program_id(0)
    context = context_ref[...]
    rows = context.shape[0] * context.shape[2]
    part = sum(
        jnp.dot(
            context[:, device].reshape(rows, context.shape[3]),
            out_ref[device],
            preferred_element_type=F32,
        )
        for device in range(AT_ONCE)
    )

    @pl.when(step == 0)
    def _():
        total[...] = part

    @pl.when(step > 0)
    def _():
        total[...] += part

    @pl.when(step == N_NEAR // AT_ONCE - 1)
    def _():
        for far in range(N_FAR):
            pieces = []
            for block in range(N_NEAR):
                first = (block * N_FAR + far) * few
                pieces.append(total[first : first + few])
            sum_ref[far] = jnp.concatenate(pieces, axis=0).astype(BF)


def head_sum(context, packed, few, head_rows):
    n_mp, _, sub, features = context.shape
    d_cols = packed.shape[2]
    return pl.pallas_call(
        functools.partial(head_sum_kernel, few),
        grid=(N_NEAR // AT_ONCE,),
        in_specs=[
            pl.BlockSpec((n_mp, AT_ONCE, sub, features), lambda g: (0, g, 0, 0)),
            pl.BlockSpec((AT_ONCE, head_rows, d_cols), lambda g: (g, 0, 0)),
        ],
        out_specs=pl.BlockSpec((N_FAR, N_NEAR * few, d_cols), lambda g: (0, 0, 0)),
        out_shape=jax.ShapeDtypeStruct((N_FAR, N_NEAR * few, d_cols), BF),
        scratch_shapes=[pltpu.VMEM((n_mp * sub, d_cols), F32)],
        compiler_params=pltpu.CompilerParams(vmem_limit_bytes=60 * 2**20),
        cost_estimate=pl.CostEstimate(
            flops=2 * n_mp * sub * features * N_NEAR * d_cols,
            bytes_accessed=4 * 2**20,
            transcendentals=0,
        ),
    )(context, packed)


def project_kernel(hidden_ref, map_ref, out_ref, ordered):
    columns = out_ref.shape[2] // AT_ONCE

    @pl.when(pl.program_id(0) == 0)
    def _():
        few = hidden_ref.shape[1] // N_NEAR
        hidden = hidden_ref[...].astype(F32)
        pieces = []
        for block in range(N_NEAR):
            for far in range(N_FAR):
                pieces.append(hidden[far, block * few : (block + 1) * few])
        ordered[...] = jnp.concatenate(pieces, axis=0).astype(BF)

    folds = map_ref.shape[2] // columns
    for device in range(AT_ONCE):
        folded = map_ref[device]
        weights = jnp.concatenate(
            [folded[:, f * columns : (f + 1) * columns] for f in range(folds)], axis=0
        )
        part = jnp.dot(ordered[...], weights, preferred_element_type=F32)
        out_ref[:, :, device * columns : (device + 1) * columns] = part.astype(
            BF
        ).reshape(out_ref.shape[:2] + (columns,))


def project(hidden, packed, first, sub, columns):
    rows = hidden.shape[0] * hidden.shape[1]
    d_cols = hidden.shape[2]
    return pl.pallas_call(
        project_kernel,
        grid=(N_NEAR // AT_ONCE,),
        in_specs=[
            pl.BlockSpec(hidden.shape, lambda g: (0, 0, 0)),
            pl.BlockSpec((AT_ONCE, columns, d_cols), lambda g: (g, first // columns, 0)),
        ],
        out_specs=pl.BlockSpec(
            (rows // sub, sub, AT_ONCE * columns), lambda g: (0, 0, g)
        ),
        out_shape=jax.ShapeDtypeStruct((rows // sub, sub, N_NEAR * columns), BF),
        scratch_shapes=[pltpu.VMEM((rows, d_cols), BF)],
        compiler_params=pltpu.CompilerParams(vmem_limit_bytes=60 * 2**20),
        cost_estimate=pl.CostEstimate(
            flops=2 * rows * d_cols * N_NEAR * columns,
            bytes_accessed=2 * 2**20,
            transcendentals=0,
        ),
    )(hidden, packed)


def attend_kernel(few, place_ref, query_ref, kv_ref, more_ref, out_ref):
    rows = query_ref.shape[0]
    heads = query_ref.shape[1] // HEAD
    total = kv_ref.shape[0] * kv_ref.shape[1]
    kv = kv_ref[...].reshape(total, 2 * HEAD)
    keys, values = kv[:, :HEAD], kv[:, HEAD:]
    query_pos = place_ref[0] * rows + lax.broadcasted_iota(
        jnp.int32, (rows, total), 0
    )
    allowed = query_pos >= lax.broadcasted_iota(jnp.int32, (rows, total), 1)
    found = []
    for head in range(heads):
        scores = lax.dot_general(
            query_ref[:, head * HEAD : (head + 1) * HEAD],
            keys,
            (((1,), (1,)), ((), ())),
            preferred_element_type=F32,
        ) * HEAD ** (-0.5)
        scores = jnp.where(allowed, scores, -jnp.inf)
        weights = jnp.exp(scores - jnp.max(scores, axis=1, keepdims=True))
        probs = (weights / jnp.sum(weights, axis=1, keepdims=True)).astype(BF)
        found.append(jnp.dot(probs, values, preferred_element_type=F32))
    context = jnp.concatenate(found, axis=1)
    for device in range(N_NEAR):
        pieces = []
        for xl in range(N_XL):
            first = (xl * N_NEAR + device) * few
            pieces.append(context[first : first + few])
        out_ref[device, :, : heads * HEAD] = jnp.concatenate(pieces, axis=0).astype(BF)
        out_ref[device, :, heads * HEAD :] = more_ref[device]


def attend(place, query, kv, more, few):
    near, sub, extra = more.shape
    total = kv.shape[0] * kv.shape[1]
    vmem = pl.BlockSpec(memory_space=pltpu.VMEM)
    return pl.pallas_call(
        functools.partial(attend_kernel, few),
        in_specs=[pl.BlockSpec(memory_space=pltpu.SMEM), vmem, vmem, vmem],
        out_specs=vmem,
        out_shape=jax.ShapeDtypeStruct((near, sub, query.shape[1] + extra), BF),
        compiler_params=pltpu.CompilerParams(vmem_limit_bytes=40 * 2**20),
        cost_estimate=pl.CostEstimate(
            flops=4 * query.shape[0] * query.shape[1] * total,
            bytes_accessed=2 * 2**20,
            transcendentals=query.shape[0] * query.shape[1] // HEAD * total,
        ),
    )(place, query, kv, more)


def weight_kernel(context_ref, grad_ref, tail_ref, out_ref):
    blocks = out_ref.shape[0]
    part = context_ref.shape[1] // blocks
    for block in range(blocks):
        out_ref[block, :part] = lax.dot_general(
            context_ref[:, block * part : (block + 1) * part],
            grad_ref[...],
            (((0,), (0,)), ((), ())),
            preferred_element_type=F32,
        ).astype(BF)
        out_ref[block, part:] = tail_ref[...]


def weight_parts(context, grad, tail):
    part = context.shape[1] // N_MP
    vmem = pl.BlockSpec(memory_space=pltpu.VMEM)
    return pl.pallas_call(
        weight_kernel,
        in_specs=[vmem] * 3,
        out_specs=vmem,
        out_shape=jax.ShapeDtypeStruct(
            (N_MP, part + tail.shape[0], tail.shape[1]), BF
        ),
        compiler_params=pltpu.CompilerParams(vmem_limit_bytes=40 * 2**20),
        cost_estimate=pl.CostEstimate(
            flops=2 * context.shape[0] * context.shape[1] * grad.shape[1],
            bytes_accessed=3 * 2**20,
            transcendentals=0,
        ),
    )(context, grad, tail)


def sum_kernel(parts_ref, out_ref):
    total = parts_ref[0].astype(F32)
    for block in range(1, parts_ref.shape[0]):
        total += parts_ref[block].astype(F32)
    out_ref[...] = jnp.broadcast_to(total.astype(BF)[None], out_ref.shape)


def weight_sum(got, part):
    blocks, _, columns = got.shape
    whole = pl.BlockSpec((blocks, part, columns), lambda g: (0, 0, 0))
    return pl.pallas_call(
        sum_kernel,
        grid=(1,),
        in_specs=[whole],
        out_specs=whole,
        out_shape=jax.ShapeDtypeStruct((blocks, part, columns), BF),
        compiler_params=pltpu.CompilerParams(vmem_limit_bytes=40 * 2**20),
        cost_estimate=pl.CostEstimate(
            flops=blocks * part * columns,
            bytes_accessed=2 * 2**20,
            transcendentals=0,
        ),
    )(got)


def on_device(
    teacher_query,
    teacher_keys,
    teacher_values,
    teacher_out,
    teacher_resid,
    distill_proj,
    student_context,
    student_resid,
    student_out,
    student_gain,
):
    far = lax.axis_index(FAR)
    near = lax.axis_index(NEAR)
    dp_index = lax.axis_index(DP)
    mp_index = lax.axis_index(MP)
    rows, query_width = teacher_query.shape
    local_heads = query_width // HEAD
    total = rows * N_MP
    sub = rows // N_NEAR
    columns = student_out.shape[1]
    width = student_context.shape[1]
    head_rows, d_cols = teacher_out.shape
    few = sub // N_XL

    folds = d_cols // columns
    folded = distill_proj.reshape(folds, columns, columns)
    folded = folded.transpose(1, 0, 2).reshape(columns, d_cols)
    packed = jnp.concatenate([teacher_out, folded], axis=0)
    packed_all = lax.all_gather(packed, NEAR, axis=0, tiled=False)

    def by_near(values):
        values = values.reshape(N_XL, N_NEAR, few, values.shape[-1])
        return values.transpose(1, 0, 2, 3).reshape(N_NEAR, sub, values.shape[-1])

    kv_start = dp_index * local_heads // (HEADS // KV_HEADS)
    key_mine = lax.dynamic_slice_in_dim(teacher_keys, kv_start * HEAD, HEAD, 1)
    value_mine = lax.dynamic_slice_in_dim(teacher_values, kv_start * HEAD, HEAD, 1)
    kv_all = to_all(jnp.concatenate([key_mine, value_mine], axis=1), MP, N_MP)
    state = student_resid.astype(F32) + jnp.dot(
        student_context, student_out, preferred_element_type=F32
    )
    gain = lax.dynamic_slice_in_dim(student_gain, dp_index * columns, columns, 0)

    half = d_cols // 2
    resid_parts = teacher_resid.reshape(N_NEAR, few, 2, half)
    resid_parts = resid_parts.transpose(0, 2, 1, 3).reshape(N_NEAR, sub, half)
    more = jnp.concatenate([by_near(state.astype(BF)), resid_parts], axis=2)
    place = jnp.full((1,), mp_index, jnp.int32)
    got = exchange(attend(place, teacher_query, kv_all, more, few), NEAR)
    state_wide = got[:, :, query_width : query_width + columns].astype(F32)
    resid_mine = got[:, :, query_width + columns :]
    resid_mine = resid_mine.reshape(N_NEAR, 2, few, half).transpose(0, 2, 1, 3)

    part = width // N_MP
    context = got[:, :, :query_width].reshape(rows, query_width)
    got = to_all(context, MP, N_MP)

    head_terms = head_sum(
        got.reshape(N_MP, N_NEAR, sub, query_width), packed_all, few, head_rows
    )
    head_terms = exchange(head_terms, FAR)
    summed = jnp.sum(head_terms.astype(F32), axis=0)
    resid_mine = resid_mine.reshape(N_NEAR * few, d_cols).astype(F32)
    hidden = (resid_mine + summed).astype(BF)
    hidden_near = to_all(hidden, FAR, N_FAR)

    partial = exchange(project(hidden_near, packed_all, head_rows, sub, columns), MP)
    target_wide = jnp.sum(partial.astype(F32), axis=0)
    target_wide = target_wide.reshape(sub, N_NEAR, columns).transpose(1, 0, 2)

    gain_wide = student_gain.reshape(N_NEAR, N_FAR, columns)
    gain_wide = lax.dynamic_slice_in_dim(gain_wide, far, 1, 1)
    gained = state_wide * gain_wide
    sums = jnp.stack(
        [
            jnp.sum(state_wide * state_wide, axis=(0, 2)),
            jnp.sum(gained * gained, axis=(0, 2)),
            jnp.sum(target_wide * gained, axis=(0, 2)),
        ]
    )
    sums = jnp.stack(split(sums)).reshape(6 * sub)
    sums = jnp.pad(sums, (0, 8 * columns - 6 * sub)).reshape(8, columns)
    here = (lax.iota(jnp.int32, N_FAR) == far)[None, :, None, None]
    sent = jnp.where(here, target_wide.astype(BF)[:, None], jnp.zeros((), BF))
    sums = jnp.broadcast_to(sums, (N_NEAR, N_FAR, 8, columns))
    sent = jnp.concatenate([sent, sums], axis=2)
    got = exchange(sent.reshape(N_FAR * N_NEAR, sub + 8, columns), DP)
    got = got.reshape(N_NEAR, N_FAR, sub + 8, columns)
    got = jnp.sum(got.astype(F32), axis=1)
    target = got[:, :sub].reshape(N_NEAR, N_XL, few, columns)
    target = target.transpose(1, 0, 2, 3).reshape(rows, columns)
    sums = got[:, sub:].reshape(N_NEAR, 8 * columns)[:, : 6 * sub]
    sums = sums.reshape(N_NEAR, 2, 3, N_XL, few).sum(axis=1)
    sums = sums.transpose(1, 2, 0, 3).reshape(3, rows)

    grad_scale = total ** (-0.5)
    inverse = lax.rsqrt(sums[0] / width + EPS)
    inner = (inverse * sums[1] - sums[2]) * (grad_scale / width)
    inverse = inverse[:, None]
    error = (state * inverse * gain - target) * grad_scale
    grad_state = inverse * error * gain - state * (inverse**3 * inner[:, None])
    gain_part = jnp.sum(error * state * inverse, axis=0)[None]
    tail = jnp.concatenate(
        [error.astype(BF), *split(gain_part), jnp.zeros((14, columns), BF)], axis=0
    )

    contract_rows = (((0,), (0,)), ((), ()))
    got = exchange(weight_parts(student_context, grad_state.astype(BF), tail), MP)
    grad_wo = exchange(weight_sum(got, part), MP).reshape(width, columns)
    error_all = got[:, part : part + rows]
    first = part + rows
    grad_gain = jnp.sum(got[:, first : first + 2].astype(F32), axis=(0, 1))

    hidden_near = hidden_near.reshape(N_MP * sub, d_cols)
    hidden_all = lax.all_gather(hidden_near, NEAR, axis=0, tiled=True)
    error_all = error_all.reshape(N_NEAR, N_ZF, N_XL, N_NEAR, few, columns)
    error_all = error_all.transpose(3, 1, 2, 0, 4, 5).reshape(total, columns)
    grad_proj = -lax.dot_general(
        hidden_all, error_all, contract_rows, preferred_element_type=F32
    )
    grad_wo, grad_proj = lax.optimization_barrier((grad_wo, grad_proj))
    return (grad_wo, grad_gain, grad_proj)


def solution(mesh):
    fine = Mesh(mesh.devices.reshape(SIZES), AXES)
    in_specs = (
        P(MP, DP),
        P(MP, None),
        P(MP, None),
        P(DP, MP),
        P(DP, MP),
        P(MP, DP),
        P(MP, None),
        P(MP, DP),
        P(None, DP),
        P(),
    )
    out_specs = (P(None, DP), P(DP), P(MP, DP))
    return jax.shard_map(
        on_device, mesh=fine, in_specs=in_specs, out_specs=out_specs, check_vma=False
    )
```

```python
import functools

import jax
import jax.numpy as jnp
from jax import lax
from jax.experimental import pallas as pl
from jax.experimental.pallas import tpu as pltpu
from jax.sharding import Mesh
from jax.sharding import PartitionSpec as P

HEADS = 64
KV_HEADS = 8
HEAD = 128
EPS = 1e-05

DP = ("zn", "zf", "xl")
MP = ("xh", "y", "core")
NEAR = ("zn",)
FAR = ("zf", "xl")
AXES = DP + MP
N_NEAR, N_XL, N_MP = 8, 2, 16
N_ZF = 16 // N_NEAR
N_FAR = N_ZF * N_XL
AT_ONCE = 4
SIZES = (N_NEAR, N_ZF, N_XL, 2, 4, 2)

BF = jnp.bfloat16
F32 = jnp.float32


def exchange(pieces, axes):
    return lax.all_to_all(pieces, axes, 0, 0, tiled=True)


def to_all(block, axes, count):
    return exchange(jnp.broadcast_to(block[None], (count,) + block.shape), axes)


def split(values):
    high = values.astype(BF)
    return high, (values - high.astype(F32)).astype(BF)


def head_sum_kernel(few, context_ref, out_ref, sum_ref, total):
    step = pl.program_id(0)
    context = context_ref[...]
    rows = context.shape[0] * context.shape[2]
    part = sum(
        jnp.dot(
            context[:, device].reshape(rows, context.shape[3]),
            out_ref[device],
            preferred_element_type=F32,
        )
        for device in range(AT_ONCE)
    )

    @pl.when(step == 0)
    def _():
        total[...] = part

    @pl.when(step > 0)
    def _():
        total[...] += part

    @pl.when(step == N_NEAR // AT_ONCE - 1)
    def _():
        for far in range(N_FAR):
            pieces = []
            for block in range(N_NEAR):
                first = (block * N_FAR + far) * few
                pieces.append(total[first : first + few])
            sum_ref[far] = jnp.concatenate(pieces, axis=0).astype(BF)


def head_sum(context, packed, few, head_rows):
    n_mp, _, sub, features = context.shape
    d_cols = packed.shape[2]
    return pl.pallas_call(
        functools.partial(head_sum_kernel, few),
        grid=(N_NEAR // AT_ONCE,),
        in_specs=[
            pl.BlockSpec((n_mp, AT_ONCE, sub, features), lambda g: (0, g, 0, 0)),
            pl.BlockSpec((AT_ONCE, head_rows, d_cols), lambda g: (g, 0, 0)),
        ],
        out_specs=pl.BlockSpec((N_FAR, N_NEAR * few, d_cols), lambda g: (0, 0, 0)),
        out_shape=jax.ShapeDtypeStruct((N_FAR, N_NEAR * few, d_cols), BF),
        scratch_shapes=[pltpu.VMEM((n_mp * sub, d_cols), F32)],
        compiler_params=pltpu.CompilerParams(vmem_limit_bytes=60 * 2**20),
        cost_estimate=pl.CostEstimate(
            flops=2 * n_mp * sub * features * N_NEAR * d_cols,
            bytes_accessed=4 * 2**20,
            transcendentals=0,
        ),
    )(context, packed)


def project_kernel(hidden_ref, map_ref, out_ref, ordered):
    columns = out_ref.shape[2] // AT_ONCE

    @pl.when(pl.program_id(0) == 0)
    def _():
        few = hidden_ref.shape[1] // N_NEAR
        hidden = hidden_ref[...].astype(F32)
        pieces = []
        for block in range(N_NEAR):
            for far in range(N_FAR):
                pieces.append(hidden[far, block * few : (block + 1) * few])
        ordered[...] = jnp.concatenate(pieces, axis=0).astype(BF)

    folds = map_ref.shape[2] // columns
    for device in range(AT_ONCE):
        folded = map_ref[device]
        weights = jnp.concatenate(
            [folded[:, f * columns : (f + 1) * columns] for f in range(folds)], axis=0
        )
        part = jnp.dot(ordered[...], weights, preferred_element_type=F32)
        out_ref[:, :, device * columns : (device + 1) * columns] = part.astype(
            BF
        ).reshape(out_ref.shape[:2] + (columns,))


def project(hidden, packed, first, sub, columns):
    rows = hidden.shape[0] * hidden.shape[1]
    d_cols = hidden.shape[2]
    return pl.pallas_call(
        project_kernel,
        grid=(N_NEAR // AT_ONCE,),
        in_specs=[
            pl.BlockSpec(hidden.shape, lambda g: (0, 0, 0)),
            pl.BlockSpec((AT_ONCE, columns, d_cols), lambda g: (g, first // columns, 0)),
        ],
        out_specs=pl.BlockSpec(
            (rows // sub, sub, AT_ONCE * columns), lambda g: (0, 0, g)
        ),
        out_shape=jax.ShapeDtypeStruct((rows // sub, sub, N_NEAR * columns), BF),
        scratch_shapes=[pltpu.VMEM((rows, d_cols), BF)],
        compiler_params=pltpu.CompilerParams(vmem_limit_bytes=60 * 2**20),
        cost_estimate=pl.CostEstimate(
            flops=2 * rows * d_cols * N_NEAR * columns,
            bytes_accessed=2 * 2**20,
            transcendentals=0,
        ),
    )(hidden, packed)


def attend_kernel(few, place_ref, query_ref, kv_ref, more_ref, out_ref):
    rows = query_ref.shape[0]
    heads = query_ref.shape[1] // HEAD
    total = kv_ref.shape[0] * kv_ref.shape[1]
    kv = kv_ref[...].reshape(total, 2 * HEAD)
    keys, values = kv[:, :HEAD], kv[:, HEAD:]
    query_pos = place_ref[0] * rows + lax.broadcasted_iota(
        jnp.int32, (rows, total), 0
    )
    allowed = query_pos >= lax.broadcasted_iota(jnp.int32, (rows, total), 1)
    found = []
    for head in range(heads):
        scores = lax.dot_general(
            query_ref[:, head * HEAD : (head + 1) * HEAD],
            keys,
            (((1,), (1,)), ((), ())),
            preferred_element_type=F32,
        ) * HEAD ** (-0.5)
        scores = jnp.where(allowed, scores, -jnp.inf)
        weights = jnp.exp(scores - jnp.max(scores, axis=1, keepdims=True))
        probs = (weights / jnp.sum(weights, axis=1, keepdims=True)).astype(BF)
        found.append(jnp.dot(probs, values, preferred_element_type=F32))
    context = jnp.concatenate(found, axis=1)
    for device in range(N_NEAR):
        pieces = []
        for xl in range(N_XL):
            first = (xl * N_NEAR + device) * few
            pieces.append(context[first : first + few])
        out_ref[device, :, : heads * HEAD] = jnp.concatenate(pieces, axis=0).astype(BF)
        out_ref[device, :, heads * HEAD :] = more_ref[device]


def attend(place, query, kv, more, few):
    near, sub, extra = more.shape
    total = kv.shape[0] * kv.shape[1]
    vmem = pl.BlockSpec(memory_space=pltpu.VMEM)
    return pl.pallas_call(
        functools.partial(attend_kernel, few),
        in_specs=[pl.BlockSpec(memory_space=pltpu.SMEM), vmem, vmem, vmem],
        out_specs=vmem,
        out_shape=jax.ShapeDtypeStruct((near, sub, query.shape[1] + extra), BF),
        compiler_params=pltpu.CompilerParams(vmem_limit_bytes=40 * 2**20),
        cost_estimate=pl.CostEstimate(
            flops=4 * query.shape[0] * query.shape[1] * total,
            bytes_accessed=2 * 2**20,
            transcendentals=query.shape[0] * query.shape[1] // HEAD * total,
        ),
    )(place, query, kv, more)


def weight_kernel(context_ref, grad_ref, tail_ref, out_ref):
    blocks = out_ref.shape[0]
    part = context_ref.shape[1] // blocks
    for block in range(blocks):
        out_ref[block, :part] = lax.dot_general(
            context_ref[:, block * part : (block + 1) * part],
            grad_ref[...],
            (((0,), (0,)), ((), ())),
            preferred_element_type=F32,
        ).astype(BF)
        out_ref[block, part:] = tail_ref[...]


def weight_parts(context, grad, tail):
    part = context.shape[1] // N_MP
    vmem = pl.BlockSpec(memory_space=pltpu.VMEM)
    return pl.pallas_call(
        weight_kernel,
        in_specs=[vmem] * 3,
        out_specs=vmem,
        out_shape=jax.ShapeDtypeStruct(
            (N_MP, part + tail.shape[0], tail.shape[1]), BF
        ),
        compiler_params=pltpu.CompilerParams(vmem_limit_bytes=40 * 2**20),
        cost_estimate=pl.CostEstimate(
            flops=2 * context.shape[0] * context.shape[1] * grad.shape[1],
            bytes_accessed=3 * 2**20,
            transcendentals=0,
        ),
    )(context, grad, tail)


def map_kernel(few, hidden_ref, error_ref, out_ref, total):
    step = pl.program_id(0)
    block = N_NEAR * N_FAR * few
    part = None
    for device in range(AT_ONCE):
        pieces = []
        for far in range(N_FAR):
            zf, xl = far // N_XL, far % N_XL
            for near in range(N_NEAR):
                pieces.append(error_ref[near * N_ZF + zf, xl, device])
        error = jnp.concatenate(pieces, axis=0).astype(BF)
        product = lax.dot_general(
            error,
            hidden_ref[device * block : (device + 1) * block],
            (((0,), (0,)), ((), ())),
            preferred_element_type=F32,
        )
        part = product if part is None else part + product

    @pl.when(step == 0)
    def _():
        total[...] = part

    @pl.when(step == N_NEAR // AT_ONCE - 1)
    def _():
        out_ref[...] = -(total[...] + part).T


def map_grad(hidden, error, few):
    rows, d_cols = hidden.shape
    columns = error.shape[-1]
    steps = N_NEAR // AT_ONCE
    return pl.pallas_call(
        functools.partial(map_kernel, few),
        grid=(steps,),
        in_specs=[
            pl.BlockSpec((rows // steps, d_cols), lambda g: (g, 0)),
            pl.BlockSpec(
                error.shape[:2] + (AT_ONCE,) + error.shape[3:],
                lambda g: (0, 0, g, 0, 0),
            ),
        ],
        out_specs=pl.BlockSpec((d_cols, columns), lambda g: (0, 0)),
        out_shape=jax.ShapeDtypeStruct((d_cols, columns), F32),
        scratch_shapes=[pltpu.VMEM((columns, d_cols), F32)],
        compiler_params=pltpu.CompilerParams(vmem_limit_bytes=12 * 2**20),
        cost_estimate=pl.CostEstimate(
            flops=2 * rows * d_cols * columns,
            bytes_accessed=4 * 2**20,
            transcendentals=0,
        ),
    )(hidden, error)


def on_device(
    teacher_query,
    teacher_keys,
    teacher_values,
    teacher_out,
    teacher_resid,
    distill_proj,
    student_context,
    student_resid,
    student_out,
    student_gain,
):
    far = lax.axis_index(FAR)
    near = lax.axis_index(NEAR)
    dp_index = lax.axis_index(DP)
    mp_index = lax.axis_index(MP)
    rows, query_width = teacher_query.shape
    local_heads = query_width // HEAD
    total = rows * N_MP
    sub = rows // N_NEAR
    columns = student_out.shape[1]
    width = student_context.shape[1]
    head_rows, d_cols = teacher_out.shape
    few = sub // N_XL

    folds = d_cols // columns
    folded = distill_proj.reshape(folds, columns, columns)
    folded = folded.transpose(1, 0, 2).reshape(columns, d_cols)
    packed = jnp.concatenate([teacher_out, folded], axis=0)
    packed_all = lax.all_gather(packed, NEAR, axis=0, tiled=False)

    def by_near(values):
        values = values.reshape(N_XL, N_NEAR, few, values.shape[-1])
        return values.transpose(1, 0, 2, 3).reshape(N_NEAR, sub, values.shape[-1])

    kv_start = dp_index * local_heads // (HEADS // KV_HEADS)
    key_mine = lax.dynamic_slice_in_dim(teacher_keys, kv_start * HEAD, HEAD, 1)
    value_mine = lax.dynamic_slice_in_dim(teacher_values, kv_start * HEAD, HEAD, 1)
    kv_all = to_all(jnp.concatenate([key_mine, value_mine], axis=1), MP, N_MP)
    state = student_resid.astype(F32) + jnp.dot(
        student_context, student_out, preferred_element_type=F32
    )
    gain = lax.dynamic_slice_in_dim(student_gain, dp_index * columns, columns, 0)

    half = d_cols // 2
    resid_parts = teacher_resid.reshape(N_NEAR, few, 2, half)
    resid_parts = resid_parts.transpose(0, 2, 1, 3).reshape(N_NEAR, sub, half)
    more = jnp.concatenate([by_near(state.astype(BF)), resid_parts], axis=2)
    place = jnp.full((1,), mp_index, jnp.int32)
    got = exchange(attend(place, teacher_query, kv_all, more, few), NEAR)
    state_wide = got[:, :, query_width : query_width + columns].astype(F32)
    resid_mine = got[:, :, query_width + columns :]
    resid_mine = resid_mine.reshape(N_NEAR, 2, few, half).transpose(0, 2, 1, 3)

    part = width // N_MP
    context = got[:, :, :query_width].reshape(rows, query_width)
    got = to_all(context, MP, N_MP)

    head_terms = head_sum(
        got.reshape(N_MP, N_NEAR, sub, query_width), packed_all, few, head_rows
    )
    head_terms = exchange(head_terms, FAR)
    summed = jnp.sum(head_terms.astype(F32), axis=0)
    resid_mine = resid_mine.reshape(N_NEAR * few, d_cols).astype(F32)
    hidden = (resid_mine + summed).astype(BF)
    hidden_near = to_all(hidden, FAR, N_FAR)

    partial = exchange(project(hidden_near, packed_all, head_rows, sub, columns), MP)
    target_wide = jnp.sum(partial.astype(F32), axis=0)
    target_wide = target_wide.reshape(sub, N_NEAR, columns).transpose(1, 0, 2)

    gain_wide = student_gain.reshape(N_NEAR, N_FAR, columns)
    gain_wide = lax.dynamic_slice_in_dim(gain_wide, far, 1, 1)
    gained = state_wide * gain_wide
    sums = jnp.stack(
        [
            jnp.sum(state_wide * state_wide, axis=(0, 2)),
            jnp.sum(gained * gained, axis=(0, 2)),
            jnp.sum(target_wide * gained, axis=(0, 2)),
        ]
    )
    sums = jnp.stack(split(sums)).reshape(6 * sub)
    sums = jnp.pad(sums, (0, 8 * columns - 6 * sub)).reshape(8, columns)
    here = (lax.iota(jnp.int32, N_FAR) == far)[None, :, None, None]
    sent = jnp.where(here, target_wide.astype(BF)[:, None], jnp.zeros((), BF))
    sums = jnp.broadcast_to(sums, (N_NEAR, N_FAR, 8, columns))
    sent = jnp.concatenate([sent, sums], axis=2)
    got = exchange(sent.reshape(N_FAR * N_NEAR, sub + 8, columns), DP)
    got = got.reshape(N_NEAR, N_FAR, sub + 8, columns)
    got = jnp.sum(got.astype(F32), axis=1)
    target = got[:, :sub].reshape(N_NEAR, N_XL, few, columns)
    target = target.transpose(1, 0, 2, 3).reshape(rows, columns)
    sums = got[:, sub:].reshape(N_NEAR, 8 * columns)[:, : 6 * sub]
    sums = sums.reshape(N_NEAR, 2, 3, N_XL, few).sum(axis=1)
    sums = sums.transpose(1, 2, 0, 3).reshape(3, rows)

    grad_scale = total ** (-0.5)
    inverse = lax.rsqrt(sums[0] / width + EPS)
    inner = (inverse * sums[1] - sums[2]) * (grad_scale / width)
    inverse = inverse[:, None]
    error = (state * inverse * gain - target) * grad_scale
    grad_state = inverse * error * gain - state * (inverse**3 * inner[:, None])
    gain_part = jnp.sum(error * state * inverse, axis=0)[None]
    tail = jnp.concatenate(
        [error.astype(BF), *split(gain_part), jnp.zeros((14, columns), BF)], axis=0
    )

    got = exchange(weight_parts(student_context, grad_state.astype(BF), tail), MP)
    grad_wo = jnp.sum(got[:, :part].astype(F32), axis=0).astype(BF)
    grad_wo = to_all(grad_wo, MP, N_MP).reshape(width, columns)
    error_all = got[:, part : part + rows]
    first = part + rows
    grad_gain = jnp.sum(got[:, first : first + 2].astype(F32), axis=(0, 1))

    hidden_near = hidden_near.reshape(N_MP * sub, d_cols)
    hidden_all = lax.all_gather(hidden_near, NEAR, axis=0, tiled=True)
    error_all = error_all.reshape(N_MP, N_XL, N_NEAR, few, columns)
    grad_proj = map_grad(hidden_all, error_all.astype(F32), few)
    grad_wo, grad_proj = lax.optimization_barrier((grad_wo, grad_proj))
    return (grad_wo, grad_gain, grad_proj)


def solution(mesh):
    fine = Mesh(mesh.devices.reshape(SIZES), AXES)
    in_specs = (
        P(MP, DP),
        P(MP, None),
        P(MP, None),
        P(DP, MP),
        P(DP, MP),
        P(MP, DP),
        P(MP, None),
        P(MP, DP),
        P(None, DP),
        P(),
    )
    out_specs = (P(None, DP), P(DP), P(MP, DP))
    return jax.shard_map(
        on_device, mesh=fine, in_specs=in_specs, out_specs=out_specs, check_vma=False
    )
```

```python
import functools

import jax
import jax.numpy as jnp
from jax import lax
from jax.experimental import pallas as pl
from jax.experimental.pallas import tpu as pltpu
from jax.sharding import Mesh
from jax.sharding import PartitionSpec as P

HEADS = 64
KV_HEADS = 8
HEAD = 128
EPS = 1e-05

DP = ("zn", "zf", "xl")
MP = ("xh", "y", "core")
NEAR = ("zn",)
FAR = ("zf", "xl")
AXES = DP + MP
N_NEAR, N_XL, N_MP = 8, 2, 16
N_ZF = 16 // N_NEAR
N_FAR = N_ZF * N_XL
AT_ONCE = 4
SIZES = (N_NEAR, N_ZF, N_XL, 2, 4, 2)

BF = jnp.bfloat16
F32 = jnp.float32


def exchange(pieces, axes):
    return lax.all_to_all(pieces, axes, 0, 0, tiled=True)


def to_all(block, axes, count):
    return exchange(jnp.broadcast_to(block[None], (count,) + block.shape), axes)


def split(values):
    high = values.astype(BF)
    return high, (values - high.astype(F32)).astype(BF)


def head_sum_kernel(few, context_ref, out_ref, sum_ref, total):
    step = pl.program_id(0)
    context = context_ref[...]
    rows = context.shape[0] * context.shape[2]
    part = sum(
        jnp.dot(
            context[:, device].reshape(rows, context.shape[3]),
            out_ref[device],
            preferred_element_type=F32,
        )
        for device in range(AT_ONCE)
    )

    @pl.when(step == 0)
    def _():
        total[...] = part

    @pl.when(step > 0)
    def _():
        total[...] += part

    @pl.when(step == N_NEAR // AT_ONCE - 1)
    def _():
        for far in range(N_FAR):
            pieces = []
            for block in range(N_NEAR):
                first = (block * N_FAR + far) * few
                pieces.append(total[first : first + few])
            sum_ref[far] = jnp.concatenate(pieces, axis=0).astype(BF)


def head_sum(context, packed, few, head_rows):
    n_mp, _, sub, features = context.shape
    d_cols = packed.shape[2]
    return pl.pallas_call(
        functools.partial(head_sum_kernel, few),
        grid=(N_NEAR // AT_ONCE,),
        in_specs=[
            pl.BlockSpec((n_mp, AT_ONCE, sub, features), lambda g: (0, g, 0, 0)),
            pl.BlockSpec((AT_ONCE, head_rows, d_cols), lambda g: (g, 0, 0)),
        ],
        out_specs=pl.BlockSpec((N_FAR, N_NEAR * few, d_cols), lambda g: (0, 0, 0)),
        out_shape=jax.ShapeDtypeStruct((N_FAR, N_NEAR * few, d_cols), BF),
        scratch_shapes=[pltpu.VMEM((n_mp * sub, d_cols), F32)],
        compiler_params=pltpu.CompilerParams(vmem_limit_bytes=60 * 2**20),
        cost_estimate=pl.CostEstimate(
            flops=2 * n_mp * sub * features * N_NEAR * d_cols,
            bytes_accessed=4 * 2**20,
            transcendentals=0,
        ),
    )(context, packed)


def project_kernel(hidden_ref, map_ref, out_ref, ordered):
    columns = out_ref.shape[2] // AT_ONCE

    @pl.when(pl.program_id(0) == 0)
    def _():
        few = hidden_ref.shape[1] // N_NEAR
        hidden = hidden_ref[...].astype(F32)
        pieces = []
        for block in range(N_NEAR):
            for far in range(N_FAR):
                pieces.append(hidden[far, block * few : (block + 1) * few])
        ordered[...] = jnp.concatenate(pieces, axis=0).astype(BF)

    folds = map_ref.shape[2] // columns
    for device in range(AT_ONCE):
        folded = map_ref[device]
        weights = jnp.concatenate(
            [folded[:, f * columns : (f + 1) * columns] for f in range(folds)], axis=0
        )
        part = jnp.dot(ordered[...], weights, preferred_element_type=F32)
        out_ref[:, :, device * columns : (device + 1) * columns] = part.astype(
            BF
        ).reshape(out_ref.shape[:2] + (columns,))


def project(hidden, packed, first, sub, columns):
    rows = hidden.shape[0] * hidden.shape[1]
    d_cols = hidden.shape[2]
    return pl.pallas_call(
        project_kernel,
        grid=(N_NEAR // AT_ONCE,),
        in_specs=[
            pl.BlockSpec(hidden.shape, lambda g: (0, 0, 0)),
            pl.BlockSpec((AT_ONCE, columns, d_cols), lambda g: (g, first // columns, 0)),
        ],
        out_specs=pl.BlockSpec(
            (rows // sub, sub, AT_ONCE * columns), lambda g: (0, 0, g)
        ),
        out_shape=jax.ShapeDtypeStruct((rows // sub, sub, N_NEAR * columns), BF),
        scratch_shapes=[pltpu.VMEM((rows, d_cols), BF)],
        compiler_params=pltpu.CompilerParams(vmem_limit_bytes=60 * 2**20),
        cost_estimate=pl.CostEstimate(
            flops=2 * rows * d_cols * N_NEAR * columns,
            bytes_accessed=2 * 2**20,
            transcendentals=0,
        ),
    )(hidden, packed)


def attend_kernel(few, place_ref, query_ref, kv_ref, more_ref, out_ref):
    rows = query_ref.shape[0]
    heads = query_ref.shape[1] // HEAD
    total = kv_ref.shape[0] * kv_ref.shape[1]
    kv = kv_ref[...].reshape(total, 2 * HEAD)
    keys, values = kv[:, :HEAD], kv[:, HEAD:]
    query_pos = place_ref[0] * rows + lax.broadcasted_iota(
        jnp.int32, (rows, total), 0
    )
    allowed = query_pos >= lax.broadcasted_iota(jnp.int32, (rows, total), 1)
    found = []
    for head in range(heads):
        scores = lax.dot_general(
            query_ref[:, head * HEAD : (head + 1) * HEAD],
            keys,
            (((1,), (1,)), ((), ())),
            preferred_element_type=F32,
        ) * HEAD ** (-0.5)
        scores = jnp.where(allowed, scores, -jnp.inf)
        weights = jnp.exp(scores - jnp.max(scores, axis=1, keepdims=True))
        probs = (weights / jnp.sum(weights, axis=1, keepdims=True)).astype(BF)
        found.append(jnp.dot(probs, values, preferred_element_type=F32))
    context = jnp.concatenate(found, axis=1)
    for device in range(N_NEAR):
        pieces = []
        for xl in range(N_XL):
            first = (xl * N_NEAR + device) * few
            pieces.append(context[first : first + few])
        out_ref[device, :, : heads * HEAD] = jnp.concatenate(pieces, axis=0).astype(BF)
        out_ref[device, :, heads * HEAD :] = more_ref[device]


def attend(place, query, kv, more, few):
    near, sub, extra = more.shape
    total = kv.shape[0] * kv.shape[1]
    vmem = pl.BlockSpec(memory_space=pltpu.VMEM)
    return pl.pallas_call(
        functools.partial(attend_kernel, few),
        in_specs=[pl.BlockSpec(memory_space=pltpu.SMEM), vmem, vmem, vmem],
        out_specs=vmem,
        out_shape=jax.ShapeDtypeStruct((near, sub, query.shape[1] + extra), BF),
        compiler_params=pltpu.CompilerParams(vmem_limit_bytes=40 * 2**20),
        cost_estimate=pl.CostEstimate(
            flops=4 * query.shape[0] * query.shape[1] * total,
            bytes_accessed=2 * 2**20,
            transcendentals=query.shape[0] * query.shape[1] // HEAD * total,
        ),
    )(place, query, kv, more)


def weight_kernel(context_ref, grad_ref, tail_ref, out_ref):
    blocks = out_ref.shape[0]
    part = context_ref.shape[1] // blocks
    for block in range(blocks):
        out_ref[block, :part] = lax.dot_general(
            context_ref[:, block * part : (block + 1) * part],
            grad_ref[...],
            (((0,), (0,)), ((), ())),
            preferred_element_type=F32,
        ).astype(BF)
        out_ref[block, part:] = tail_ref[...]


def weight_parts(context, grad, tail):
    part = context.shape[1] // N_MP
    vmem = pl.BlockSpec(memory_space=pltpu.VMEM)
    return pl.pallas_call(
        weight_kernel,
        in_specs=[vmem] * 3,
        out_specs=vmem,
        out_shape=jax.ShapeDtypeStruct(
            (N_MP, part + tail.shape[0], tail.shape[1]), BF
        ),
        compiler_params=pltpu.CompilerParams(vmem_limit_bytes=40 * 2**20),
        cost_estimate=pl.CostEstimate(
            flops=2 * context.shape[0] * context.shape[1] * grad.shape[1],
            bytes_accessed=3 * 2**20,
            transcendentals=0,
        ),
    )(context, grad, tail)


def map_kernel(few, hidden_ref, error_ref, out_ref, total):
    step = pl.program_id(0)
    block = N_NEAR * N_FAR * few
    part = None
    for device in range(AT_ONCE):
        pieces = []
        for far in range(N_FAR):
            zf, xl = far // N_XL, far % N_XL
            for near in range(N_NEAR):
                pieces.append(error_ref[near * N_ZF + zf, xl, device])
        error = jnp.concatenate(pieces, axis=0).astype(BF)
        product = lax.dot_general(
            error,
            hidden_ref[device * block : (device + 1) * block],
            (((0,), (0,)), ((), ())),
            preferred_element_type=F32,
        )
        part = product if part is None else part + product

    @pl.when(step == 0)
    def _():
        total[...] = part

    @pl.when(step == N_NEAR // AT_ONCE - 1)
    def _():
        out_ref[...] = -(total[...] + part).T


def map_grad(hidden, error, few):
    rows, d_cols = hidden.shape
    columns = error.shape[-1]
    steps = N_NEAR // AT_ONCE
    return pl.pallas_call(
        functools.partial(map_kernel, few),
        grid=(steps,),
        in_specs=[
            pl.BlockSpec((rows // steps, d_cols), lambda g: (g, 0)),
            pl.BlockSpec(
                error.shape[:2] + (AT_ONCE,) + error.shape[3:],
                lambda g: (0, 0, g, 0, 0),
            ),
        ],
        out_specs=pl.BlockSpec((d_cols, columns), lambda g: (0, 0)),
        out_shape=jax.ShapeDtypeStruct((d_cols, columns), F32),
        scratch_shapes=[pltpu.VMEM((columns, d_cols), F32)],
        compiler_params=pltpu.CompilerParams(vmem_limit_bytes=12 * 2**20),
        cost_estimate=pl.CostEstimate(
            flops=2 * rows * d_cols * columns,
            bytes_accessed=4 * 2**20,
            transcendentals=0,
        ),
    )(hidden, error)


def pack_kernel(out_ref, map_ref, packed_ref):
    head_rows, d_cols = out_ref.shape
    columns = map_ref.shape[1]
    packed_ref[:head_rows] = out_ref[...]
    for fold in range(d_cols // columns):
        lanes = slice(fold * columns, (fold + 1) * columns)
        packed_ref[head_rows:, lanes] = map_ref[lanes]


def pack(teacher_out, distill_proj):
    head_rows, d_cols = teacher_out.shape
    vmem = pl.BlockSpec(memory_space=pltpu.VMEM)
    return pl.pallas_call(
        pack_kernel,
        in_specs=[vmem] * 2,
        out_specs=vmem,
        out_shape=jax.ShapeDtypeStruct(
            (head_rows + distill_proj.shape[1], d_cols), BF
        ),
        compiler_params=pltpu.CompilerParams(vmem_limit_bytes=60 * 2**20),
    )(teacher_out, distill_proj)


def on_device(
    teacher_query,
    teacher_keys,
    teacher_values,
    teacher_out,
    teacher_resid,
    distill_proj,
    student_context,
    student_resid,
    student_out,
    student_gain,
):
    far = lax.axis_index(FAR)
    near = lax.axis_index(NEAR)
    dp_index = lax.axis_index(DP)
    mp_index = lax.axis_index(MP)
    rows, query_width = teacher_query.shape
    local_heads = query_width // HEAD
    total = rows * N_MP
    sub = rows // N_NEAR
    columns = student_out.shape[1]
    width = student_context.shape[1]
    head_rows, d_cols = teacher_out.shape
    few = sub // N_XL

    packed = pack(teacher_out, distill_proj)
    packed_all = lax.all_gather(packed, NEAR, axis=0, tiled=False)

    def by_near(values):
        values = values.reshape(N_XL, N_NEAR, few, values.shape[-1])
        return values.transpose(1, 0, 2, 3).reshape(N_NEAR, sub, values.shape[-1])

    kv_start = dp_index * local_heads // (HEADS // KV_HEADS)
    key_mine = lax.dynamic_slice_in_dim(teacher_keys, kv_start * HEAD, HEAD, 1)
    value_mine = lax.dynamic_slice_in_dim(teacher_values, kv_start * HEAD, HEAD, 1)
    kv_all = to_all(jnp.concatenate([key_mine, value_mine], axis=1), MP, N_MP)
    state = student_resid.astype(F32) + jnp.dot(
        student_context, student_out, preferred_element_type=F32
    )
    gain = lax.dynamic_slice_in_dim(student_gain, dp_index * columns, columns, 0)

    half = d_cols // 2
    resid_parts = teacher_resid.reshape(N_NEAR, few, 2, half)
    resid_parts = resid_parts.transpose(0, 2, 1, 3).reshape(N_NEAR, sub, half)
    more = jnp.concatenate([by_near(state.astype(BF)), resid_parts], axis=2)
    place = jnp.full((1,), mp_index, jnp.int32)
    got = exchange(attend(place, teacher_query, kv_all, more, few), NEAR)
    state_wide = got[:, :, query_width : query_width + columns].astype(F32)
    resid_mine = got[:, :, query_width + columns :]
    resid_mine = resid_mine.reshape(N_NEAR, 2, few, half).transpose(0, 2, 1, 3)

    part = width // N_MP
    context = got[:, :, :query_width].reshape(rows, query_width)
    got = to_all(context, MP, N_MP)

    head_terms = head_sum(
        got.reshape(N_MP, N_NEAR, sub, query_width), packed_all, few, head_rows
    )
    head_terms = exchange(head_terms, FAR)
    summed = jnp.sum(head_terms.astype(F32), axis=0)
    resid_mine = resid_mine.reshape(N_NEAR * few, d_cols).astype(F32)
    hidden = (resid_mine + summed).astype(BF)
    hidden_near = to_all(hidden, FAR, N_FAR)

    partial = exchange(project(hidden_near, packed_all, head_rows, sub, columns), MP)
    target_wide = jnp.sum(partial.astype(F32), axis=0)
    target_wide = target_wide.reshape(sub, N_NEAR, columns).transpose(1, 0, 2)

    gain_wide = student_gain.reshape(N_NEAR, N_FAR, columns)
    gain_wide = lax.dynamic_slice_in_dim(gain_wide, far, 1, 1)
    gained = state_wide * gain_wide
    sums = jnp.stack(
        [
            jnp.sum(state_wide * state_wide, axis=(0, 2)),
            jnp.sum(gained * gained, axis=(0, 2)),
            jnp.sum(target_wide * gained, axis=(0, 2)),
        ]
    )
    sums = jnp.stack(split(sums)).reshape(6 * sub)
    sums = jnp.pad(sums, (0, 8 * columns - 6 * sub)).reshape(8, columns)
    here = (lax.iota(jnp.int32, N_FAR) == far)[None, :, None, None]
    sent = jnp.where(here, target_wide.astype(BF)[:, None], jnp.zeros((), BF))
    sums = jnp.broadcast_to(sums, (N_NEAR, N_FAR, 8, columns))
    sent = jnp.concatenate([sent, sums], axis=2)
    got = exchange(sent.reshape(N_FAR * N_NEAR, sub + 8, columns), DP)
    got = got.reshape(N_NEAR, N_FAR, sub + 8, columns)
    got = jnp.sum(got.astype(F32), axis=1)
    target = got[:, :sub].reshape(N_NEAR, N_XL, few, columns)
    target = target.transpose(1, 0, 2, 3).reshape(rows, columns)
    sums = got[:, sub:].reshape(N_NEAR, 8 * columns)[:, : 6 * sub]
    sums = sums.reshape(N_NEAR, 2, 3, N_XL, few).sum(axis=1)
    sums = sums.transpose(1, 2, 0, 3).reshape(3, rows)

    grad_scale = total ** (-0.5)
    inverse = lax.rsqrt(sums[0] / width + EPS)
    inner = (inverse * sums[1] - sums[2]) * (grad_scale / width)
    inverse = inverse[:, None]
    error = (state * inverse * gain - target) * grad_scale
    grad_state = inverse * error * gain - state * (inverse**3 * inner[:, None])
    gain_part = jnp.sum(error * state * inverse, axis=0)[None]
    tail = jnp.concatenate(
        [error.astype(BF), *split(gain_part), jnp.zeros((14, columns), BF)], axis=0
    )

    got = exchange(weight_parts(student_context, grad_state.astype(BF), tail), MP)
    grad_wo = jnp.sum(got[:, :part].astype(F32), axis=0).astype(BF)
    grad_wo = to_all(grad_wo, MP, N_MP).reshape(width, columns)
    error_all = got[:, part : part + rows]
    first = part + rows
    grad_gain = jnp.sum(got[:, first : first + 2].astype(F32), axis=(0, 1))

    hidden_near = hidden_near.reshape(N_MP * sub, d_cols)
    hidden_all = lax.all_gather(hidden_near, NEAR, axis=0, tiled=True)
    error_all = error_all.reshape(N_MP, N_XL, N_NEAR, few, columns)
    grad_proj = map_grad(hidden_all, error_all.astype(F32), few)
    grad_wo, grad_proj = lax.optimization_barrier((grad_wo, grad_proj))
    return (grad_wo, grad_gain, grad_proj)


def solution(mesh):
    fine = Mesh(mesh.devices.reshape(SIZES), AXES)
    in_specs = (
        P(MP, DP),
        P(MP, None),
        P(MP, None),
        P(DP, MP),
        P(DP, MP),
        P(MP, DP),
        P(MP, None),
        P(MP, DP),
        P(None, DP),
        P(),
    )
    out_specs = (P(None, DP), P(DP), P(MP, DP))
    return jax.shard_map(
        on_device, mesh=fine, in_specs=in_specs, out_specs=out_specs, check_vma=False
    )
```
